32 devices in a mesh: grp: 4 (over y, x), dp: 8 (over z, core).
Axes of the slice: x: 2, y: 2, z: 4, core: 2. Of those that a mesh axis runs over, the one named last changes fastest.
Arguments:
- blocks: bfloat16 [128, 128, 1280], P(('grp', 'dp')), may hold values from -6 to 6
- cotangent: bfloat16 [128, 128, 1280], P(('grp', 'dp')), may hold values from -6 to 6
- modality: int32 [128], P(('grp', 'dp')), may hold values from 0 to 1, as said below
- time_rank: int32 [128], P(('grp', 'dp')), may hold values from 0 to 3, as said below
- qkv_weight: bfloat16 [2, 1280, 1920], P(None, 'dp'), may hold values from -5 to 5
- out_weight: bfloat16 [2, 640, 1280], P(None, 'dp'), may hold values from -0.25 to 0.25
- norm_gain: bfloat16 [2, 1280], P(None, 'dp'), may hold values from 0.5 to 1.5
Outputs:
- encoded: bfloat16 [128, 128, 1280], P(('grp', 'dp'))
- block_grad: bfloat16 [128, 128, 1280], P(('grp', 'dp'))
- qkv_grad: float32 [4, 1280, 1920], P('grp', 'dp')
- out_grad: float32 [4, 640, 1280], P('grp', 'dp')
- gain_grad: float32 [4, 1280], P('grp', 'dp')
The draws below stay inside these ranges and needn't reach their ends.
Inputs may be any that keep to these rules, and one draw needn't show every extreme that they name: On one index of dp, chosen by the draw, all blocks of all four grp rows have the same modality. `time_rank`: within each device's 4 blocks, a permutation of 0 to 3.
All inputs are finite; a program needn't handle non-finite values.
Results may differ from the reference program's by a relative error of at most 0.029.
The reference program's roundings to bfloat16 on the way count: a program that leaves them out, or rounds other values in their place, can miss the bound.
Values may be sent and summed in bfloat16 or wider, within the bound.
No kernel may reach another device: no remote copies, remote signals or barrier semaphores. Data moves between devices by JAX's collectives and lax.ppermute only.
A program may use at most 128 MiB of HBM per device.

```python
import math
import jax
import jax.numpy as jnp
from jax import lax

D = 1280
A_HEADS = 10
A_SIZE = 64
V_HEADS = 8
V_SIZE = 80
INNER = 640
WIN = 128
VWIN = 64
NB = 4
NBLK = 128
N_GRP = 4
N_DP = 8


def draw_modality(key, part):
    key = jax.random.fold_in(key, 11)
    key_row, key_kind, key_base = jax.random.split(key, 3)
    chosen = jax.random.randint(key_row, (), 0, N_DP)
    fixed_kind = jax.random.randint(key_kind, (), 0, 2)
    base = jax.random.randint(key_base, (NBLK,), 0, 2)
    device_dp = jnp.arange(NBLK) // NB % N_DP
    return jnp.where(device_dp == chosen, fixed_kind, base).astype(jnp.int32)


def draw_time_rank(key, part):
    key = jax.random.fold_in(key, 23)
    owner_keys = jax.random.split(key, NBLK // NB)
    ranks = jax.vmap(lambda one_key: jax.random.permutation(one_key, NB))(owner_keys)
    return ranks.reshape(-1).astype(jnp.int32)


def draw_blocks(key, part):
    key = jax.random.fold_in(key, 5)
    array_shape = (NBLK, WIN, D)
    values_drawn = jax.random.truncated_normal(key, -6.0, 6.0, array_shape, jnp.float32)
    pair_count = max(1, VWIN // 8)
    position = jnp.arange(WIN)
    in_window = position % VWIN
    copied = (in_window >= VWIN // 2) & (in_window < VWIN // 2 + pair_count)
    source = jnp.where(copied, position - VWIN // 2, position)
    partner = jnp.take(values_drawn, source, axis=1)
    leading = jnp.arange(D) < D // 2
    chosen = copied[:, None] & leading[None, :]
    return jnp.where(chosen[None, :, :], partner, values_drawn).astype(jnp.bfloat16)


def draw_qkv_weight(key, part):
    key = jax.random.fold_in(key, 7)
    key_drawn, key_common, key_noise = jax.random.split(key, 3)
    columns = 3 * INNER
    drawn = jax.random.truncated_normal(key_drawn, -4.0, 4.0, (2, D, columns), jnp.float32) / math.sqrt(D)
    common = jax.random.truncated_normal(key_common, -4.0, 4.0, (2, D, INNER), jnp.float32)
    noise_part = jax.random.truncated_normal(key_noise, -4.0, 4.0, (2, D, columns), jnp.float32) * (0.3 / math.sqrt(D))
    strength = jnp.array([2.0, 2.3], jnp.float32)
    column_index = jnp.arange(columns)
    within = column_index % INNER
    head_width = jnp.array([A_SIZE, V_SIZE], jnp.int32)
    aligned = (column_index[None, :] < 2 * INNER) & (within[None, :] < head_width[:, None])
    leading = (jnp.arange(D) < D // 2).astype(jnp.float32)
    common_full = jnp.take(common, within, axis=2)
    strong = strength[:, None, None] * common_full * leading[None, :, None] / math.sqrt(D // 2) + noise_part
    result = jnp.where(aligned[:, None, :], strong, drawn)
    return jnp.clip(result, -5.0, 5.0).astype(jnp.bfloat16)


def steps_of(stream_key, extent, pieces, least, top_value):
    level, own = 1.0, jax.random.fold_in(stream_key, 6)
    for dim, blocks in pieces:
        draws = jnp.exp(jax.random.uniform(jax.random.fold_in(own, dim), (blocks,), jnp.float32, least / len(pieces), top_value / len(pieces)))
        level = level * jnp.repeat(draws, extent[dim] // blocks).reshape([-1 if axis == dim else 1 for axis in range(len(extent))])
    return level


def gaussian(own_key, dims, spread, bound, cuts=(), held_as=jnp.bfloat16):
    entries = spread * jax.random.normal(own_key, dims, jnp.float32)
    if cuts:
        entries = entries * steps_of(own_key, dims, cuts, -0.22, 0.18)
    return jnp.clip(entries, -bound, bound).astype(held_as)


def setup_inputs(seed: int = 0) -> dict:
    streams_of = jax.random.split(jax.random.key(seed), 8)
    return {
        "blocks": draw_blocks(jax.random.fold_in(streams_of[7], 71), 0),
        "cotangent": gaussian(streams_of[1], (NBLK, WIN, D), 1.0, 6.0, ((0, 32),)),
        "modality": draw_modality(jax.random.fold_in(streams_of[7], 71), 0),
        "time_rank": draw_time_rank(jax.random.fold_in(streams_of[7], 71), 0),
        "qkv_weight": draw_qkv_weight(jax.random.fold_in(streams_of[7], 71), 0),
        "out_weight": gaussian(streams_of[5], (2, INNER, D), INNER ** -0.5, 0.25, ((1, 8),)),
        "norm_gain": jnp.clip(1.0 + 0.1 * jax.random.normal(streams_of[6], (2, D), jnp.float32), 0.5, 1.5).astype(jnp.bfloat16),
    }


EPSILON = 1e-05

def attend(qkv_rows, out_cot, heads, head_size, window):
    total_rows = qkv_rows.shape[0]
    inner = heads * head_size
    windows = total_rows // window
    shape = (windows, window, heads, head_size)
    query = qkv_rows[:, :inner].reshape(shape).astype(jnp.float32)
    keys = qkv_rows[:, inner:2 * inner].reshape(shape).astype(jnp.float32)
    values = qkv_rows[:, 2 * inner:].reshape(shape).astype(jnp.float32)
    scale = 1.0 / math.sqrt(head_size)
    scores = jnp.einsum('wqhd,wkhd->whqk', query, keys) * scale
    row_max = lax.optimization_barrier(jnp.max(scores, axis=-1, keepdims=True))
    exponent = jnp.exp(scores - row_max)
    probs = exponent / lax.optimization_barrier(jnp.sum(exponent, axis=-1, keepdims=True))
    probs_low = probs.astype(jnp.bfloat16)
    probs_wide = probs_low.astype(jnp.float32)
    mixed = jnp.einsum('whqk,wkhd->wqhd', probs_wide, values).astype(jnp.bfloat16).reshape(total_rows, inner)
    cot_heads = out_cot.reshape(shape).astype(jnp.float32)
    d_probs = jnp.einsum('wqhd,wkhd->whqk', cot_heads, values)
    d_values = jnp.einsum('whqk,wqhd->wkhd', probs_wide, cot_heads).astype(jnp.bfloat16)
    d_scores = (probs * (d_probs - lax.optimization_barrier(jnp.sum(d_probs * probs, axis=-1, keepdims=True))) * scale).astype(jnp.bfloat16)
    d_wide = d_scores.astype(jnp.float32)
    d_query = jnp.einsum('whqk,wkhd->wqhd', d_wide, keys).astype(jnp.bfloat16)
    d_keys = jnp.einsum('whqk,wqhd->wkhd', d_wide, query).astype(jnp.bfloat16)
    d_qkv = jnp.concatenate([d_query.reshape(total_rows, inner), d_keys.reshape(total_rows, inner), d_values.reshape(total_rows, inner)], axis=1)
    return (mixed, d_qkv)

def audio_attend(qkv_rows, out_cot):
    return attend(qkv_rows, out_cot, A_HEADS, A_SIZE, WIN)

def vision_attend(qkv_rows, out_cot):
    return attend(qkv_rows, out_cot, V_HEADS, V_SIZE, VWIN)

def encode(x_rows, cot_rows, w_qkv, w_out, gain, kind_index):
    x_float = x_rows.astype(jnp.float32)
    mean_row = lax.optimization_barrier(jnp.mean(x_float, axis=-1, keepdims=True))
    centered = x_float - mean_row
    inverse = lax.rsqrt(lax.optimization_barrier(jnp.mean(centered * centered, axis=-1, keepdims=True)) + EPSILON)
    x_hat = centered * inverse
    gain_float = gain.astype(jnp.float32)
    normed = (x_hat * gain_float).astype(jnp.bfloat16)
    qkv_rows = jnp.dot(normed, w_qkv, preferred_element_type=jnp.float32).astype(jnp.bfloat16)
    d_attn = jnp.dot(cot_rows, w_out.T, preferred_element_type=jnp.float32).astype(jnp.bfloat16)
    mixed, d_qkv = lax.cond(kind_index == 0, audio_attend, vision_attend, qkv_rows, d_attn)
    output = (x_float + jnp.dot(mixed, w_out, preferred_element_type=jnp.float32)).astype(jnp.bfloat16)
    grad_out = jnp.dot(mixed.T, cot_rows, preferred_element_type=jnp.float32)
    grad_qkv = jnp.dot(normed.T, d_qkv, preferred_element_type=jnp.float32)
    d_normed = jnp.dot(d_qkv, w_qkv.T, preferred_element_type=jnp.float32)
    grad_gain = lax.optimization_barrier(jnp.sum(d_normed * x_hat, axis=0))
    scaled = d_normed * gain_float
    d_input = inverse * (scaled - lax.optimization_barrier(jnp.mean(scaled, axis=-1, keepdims=True)) - x_hat * lax.optimization_barrier(jnp.mean(scaled * x_hat, axis=-1, keepdims=True)))
    input_grad = (cot_rows.astype(jnp.float32) + d_input).astype(jnp.bfloat16)
    return (output, input_grad, grad_qkv, grad_out, grad_gain)

def reference(blocks, cotangent, modality, time_rank, qkv_weight, out_weight, norm_gain):

    def one_block(carry, item):
        x_rows, cot_rows, kind_index = item
        output, input_grad, grad_qkv, grad_out, grad_gain = encode(x_rows, cot_rows, qkv_weight[kind_index], out_weight[kind_index], norm_gain[kind_index], kind_index)
        carry = (carry[0].at[kind_index].add(grad_qkv), carry[1].at[kind_index].add(grad_out), carry[2].at[kind_index].add(grad_gain))
        return (carry, (output, input_grad))
    start = (jnp.zeros((2, D, 3 * INNER), jnp.float32), jnp.zeros((2, INNER, D), jnp.float32), jnp.zeros((2, D), jnp.float32))
    totals, (outputs, input_grads) = lax.scan(one_block, start, (blocks, cotangent, modality))
    owners = N_GRP * N_DP
    ranks = time_rank.reshape(owners, NB)

    def place(rank_row, values):
        return jnp.zeros_like(values).at[rank_row].set(values)
    encoded = jax.vmap(place)(ranks, outputs.reshape(owners, NB, WIN, D)).reshape(NBLK, WIN, D)
    block_grad = jax.vmap(place)(ranks, input_grads.reshape(owners, NB, WIN, D)).reshape(NBLK, WIN, D)
    select = jnp.arange(N_GRP) // 2
    return (encoded, block_grad, totals[0][select], totals[1][select], totals[2][select])
```

```python
import functools
import math

import jax
import jax.numpy as jnp
from jax import lax
from jax.experimental import pallas as pl
from jax.experimental.pallas import tpu as pltpu
from jax.sharding import PartitionSpec as P

A_HEADS = 10
A_SIZE = 64
V_HEADS = 8
V_SIZE = 80
VWIN = 64
EPSILON = 1e-05
LANES = 128
AXES = ("grp", "dp")
VMEM_LIMIT = 60 * 1024 * 1024
BF16 = jnp.bfloat16
F32 = jnp.float32

VMEM = pl.BlockSpec(memory_space=pltpu.VMEM)
SMEM = pl.BlockSpec(memory_space=pltpu.SMEM)
HBM = pl.BlockSpec(memory_space=pl.ANY)


def params():
    return pltpu.CompilerParams(vmem_limit_bytes=VMEM_LIMIT)


def cost(flops, traffic):
    return pl.CostEstimate(flops=flops, bytes_accessed=traffic, transcendentals=0)


def dot_nn(a, b):
    return lax.dot_general(a, b, (((1,), (0,)), ((), ())), preferred_element_type=F32)


def dot_nt(a, b):
    return lax.dot_general(a, b, (((1,), (1,)), ((), ())), preferred_element_type=F32)


def dot_tn(a, b):
    return lax.dot_general(a, b, (((0,), (0,)), ((), ())), preferred_element_type=F32)


def normalise(x):
    mean = jnp.mean(x, axis=-1, keepdims=True)
    centered = x - mean
    inverse = lax.rsqrt(jnp.mean(centered * centered, axis=-1, keepdims=True) + EPSILON)
    return centered * inverse, inverse


def norm_kernel(kind_ref, x_ref, gain_ref, h_ref, ht_ref):
    def body(b, carry):
        x_hat, _ = normalise(x_ref[b].astype(F32))
        h = (x_hat * gain_ref[pl.ds(kind_ref[b], 1), :]).astype(BF16)
        h_ref[b] = h
        ht_ref[b] = h.T
        return carry

    lax.fori_loop(0, x_ref.shape[0], body, 0)


def attend(b, heads, size, window, qkv, da, attnt_ref, dq_ref, dk_ref, dv_ref):
    rows = qkv.shape[0]
    inner = heads * size
    scale = 1.0 / math.sqrt(size)
    same = None
    if window < rows:
        key = lax.broadcasted_iota(jnp.int32, (rows, 2 * rows), 0) // window
        query = lax.broadcasted_iota(jnp.int32, (rows, 2 * rows), 1) % rows // window
        same = key == query
    sums = {}

    def add(name, tile, value):
        known = sums.get((name, tile))
        sums[name, tile] = value if known is None else known + value

    for head in range(0, heads, 2):
        first, last = head * size // LANES, ((head + 2) * size - 1) // LANES + 1
        low, wide = first * LANES, (last - first) * LANES
        lane = lax.broadcasted_iota(jnp.int32, (rows, wide), 1) + low
        row = lax.broadcasted_iota(jnp.int32, (wide, rows), 0) + low
        lanes = [(lane >= h * size) & (lane < (h + 1) * size) for h in (head, head + 1)]
        bands = [(row >= h * size) & (row < (h + 1) * size) for h in (head, head + 1)]
        q, k, v = (qkv[:, at + low : at + low + wide] for at in (0, inner, 2 * inner))
        g = da[:, low : low + wide]
        q_pair = jnp.concatenate([jnp.where(mask, q, 0) for mask in lanes], axis=0)
        g_pair = jnp.concatenate([jnp.where(mask, g, 0) for mask in lanes], axis=0)
        scores = dot_nt(k, q_pair) * scale
        if same is not None:
            scores = jnp.where(same, scores, -1e30)
        exponent = jnp.exp(scores - jnp.max(scores, axis=0, keepdims=True))
        probs = exponent * (1.0 / jnp.sum(exponent, axis=0, keepdims=True))
        d_probs = dot_nt(v, g_pair)
        mean = jnp.sum(d_probs * probs, axis=0, keepdims=True)
        d_scores = (probs * (d_probs - mean) * scale).astype(BF16)
        probs = probs.astype(BF16)
        d_v = dot_nn(probs, g_pair)
        d_k = dot_nn(d_scores, q_pair)
        vt, kt = v.T, k.T
        mixed = dot_nn(
            jnp.concatenate([jnp.where(band, vt, 0) for band in bands], axis=1),
            jnp.concatenate([probs[:, :rows], probs[:, rows:]], axis=0),
        )
        d_q = dot_nn(
            jnp.concatenate([jnp.where(band, kt, 0) for band in bands], axis=1),
            jnp.concatenate([d_scores[:, :rows], d_scores[:, rows:]], axis=0),
        )
        for tile in range(first, last):
            span = slice(tile * LANES - low, (tile + 1) * LANES - low)
            add("v", tile, d_v[:, span])
            add("k", tile, d_k[:, span])
            add("q", tile, d_q[span])
            add("o", tile, mixed[span])
        for tile in range(first, last):
            span = slice(tile * LANES, (tile + 1) * LANES)
            if (head + 2) * size >= (tile + 1) * LANES:
                dv_ref[b, :, span] = sums.pop(("v", tile)).astype(BF16)
                dk_ref[b, :, span] = sums.pop(("k", tile)).astype(BF16)
                dq_ref[b, :, span] = sums.pop(("q", tile)).astype(BF16).T
                attnt_ref[b, span, :] = sums.pop(("o", tile)).astype(BF16)


def piece_copies(listed, wq, wo, sems):
    copies = []

    def add(source, target):
        copies.append(pltpu.make_async_copy(source, target, sems.at[len(copies)]))

    half_rows = listed[0][0].shape[1]
    wide = wq.shape[2]
    narrow = wo.shape[2] // 2
    for ref, at, kind, half, shard in listed:
        row = pl.multiple_of((shard * 2 + half) * half_rows, 16)
        out_row = pl.multiple_of(shard * half_rows, 16)
        column = pl.multiple_of(half * narrow, LANES)
        add(ref.at[at, :, pl.ds(0, wide)], wq.at[kind, pl.ds(row, half_rows), :])
        add(
            ref.at[at, :, pl.ds(wide, narrow)],
            wo.at[kind, pl.ds(out_row, half_rows), pl.ds(column, narrow)],
        )
    return copies


def routed_entries(where_ref, refs):
    g, z, c = where_ref[0], where_ref[1], where_ref[2]
    cores = (c, 1 - c)
    listed = []

    def add(ref, at, q, shard):
        listed.append((ref, at, q // 2, q % 2, shard))

    for ref, core in zip(refs[:2], cores):
        for q in range(4):
            add(ref, q, q, 2 * z + core)
    for i, far in ((2, 3), (4, 2)):
        for ref, core in zip(refs[i : i + 2], cores):
            for other in range(4):
                add(ref, other, g ^ other, 2 * lax.rem(z + far, 4) + core)
    for other in range(4):
        for ref, core in zip(refs[6 + 2 * other : 8 + 2 * other], cores):
            add(ref, 0, g ^ other, 2 * lax.rem(z + 1, 4) + core)
    return listed


def load_weights(routed, where_ref, refs, wq, wo, sems):
    if routed:
        copies = piece_copies(routed_entries(where_ref, refs), wq, wo, sems)
    else:
        copies = [
            pltpu.make_async_copy(refs[0], wq, sems.at[0]),
            pltpu.make_async_copy(refs[1], wo, sems.at[1]),
        ]
    for copy in copies:
        copy.start()
    for copy in copies:
        copy.wait()


def layer_kernel(routed, n_weights, where_ref, kind_ref, h_ref, cot_ref, *rest):
    weights, rest = rest[:n_weights], rest[n_weights:]
    attnt_ref, dq_ref, dk_ref, dv_ref, wq, wo, qkv_ref, da_ref, sems = rest
    load_weights(routed, where_ref, weights, wq, wo, sems)
    chunk = 3 * LANES

    def body(b, carry):
        kind = kind_ref[b]
        for at in range(0, wq.shape[2], chunk):
            qkv_ref[:, at : at + chunk] = dot_nn(h_ref[b], wq[kind, :, at : at + chunk]).astype(BF16)
        for at in range(0, wo.shape[1], LANES):
            da_ref[:, at : at + LANES] = dot_nt(cot_ref[b], wo[kind, at : at + LANES, :]).astype(BF16)

        @pl.when(kind == 0)
        def _():
            attend(b, A_HEADS, A_SIZE, qkv_ref.shape[0], qkv_ref, da_ref, attnt_ref, dq_ref, dk_ref, dv_ref)

        @pl.when(kind != 0)
        def _():
            attend(b, V_HEADS, V_SIZE, VWIN, qkv_ref, da_ref, attnt_ref, dq_ref, dk_ref, dv_ref)

        return carry

    lax.fori_loop(0, h_ref.shape[0], body, 0)


def result_kernel(routed, n_weights, where_ref, kind_ref, rank_ref, x_ref, cot_ref, gain_ref, attnt_ref, dq_ref, dk_ref, dv_ref, *rest):
    weights, rest = rest[:n_weights], rest[n_weights:]
    encoded_ref, grad_ref, wq, wo, wide_ref, sems = rest
    load_weights(routed, where_ref, weights, wq, wo, sems)
    inner = dq_ref.shape[2]
    chunk = 2 * LANES
    width = x_ref.shape[2]

    def body(b, carry):
        kind, rank = kind_ref[b], rank_ref[b]
        attn = attnt_ref[b].T
        for at in range(0, width, chunk):
            span = slice(at, at + chunk)
            encoded_ref[rank, :, span] = (
                x_ref[b, :, span].astype(F32) + dot_nn(attn, wo[kind, :, span])
            ).astype(BF16)
            wide_ref[:, span] = (
                dot_nt(dq_ref[b], wq[kind, span, :inner])
                + dot_nt(dk_ref[b], wq[kind, span, inner : 2 * inner])
                + dot_nt(dv_ref[b], wq[kind, span, 2 * inner :])
            )
        x_hat, inverse = normalise(x_ref[b].astype(F32))
        scaled = wide_ref[...] * gain_ref[pl.ds(kind, 1), :]
        d_input = inverse * (
            scaled
            - jnp.mean(scaled, axis=-1, keepdims=True)
            - x_hat * jnp.mean(scaled * x_hat, axis=-1, keepdims=True)
        )
        grad_ref[rank] = (cot_ref[b].astype(F32) + d_input).astype(BF16)
        return carry

    lax.fori_loop(0, x_ref.shape[0], body, 0)


def left_kernel(where_ref, kind_ref, ht_a, ht_b, left):
    g, c = where_ref[0], where_ref[2]
    count = ht_a.shape[0]
    rows = left.shape[2] // 8
    for far in range(2):
        kind = (g // 2) ^ far
        for i in range(2 * count):
            source = ht_a if i < count else ht_b
            keep = kind_ref[i] == kind
            for side in range(2):
                for z in range(4):
                    row = pl.multiple_of(((2 * z + c) * 2 + ((g % 2) ^ side)) * rows, 16)
                    value = source[i % count, pl.ds(row, rows), :]
                    at = (side * 4 + z) * rows
                    left[far, i // count, at : at + rows, (i % count) * LANES : (i % count + 1) * LANES] = (
                        jnp.where(keep, value, jnp.zeros_like(value))
                    )


def store(far, side, chunk, second, value, cut, refs):
    y_ref, x_ref, own_ref, xa_ref, yb_ref = refs
    size = value.shape[-1]
    span = slice(chunk * size, (chunk + 1) * size)
    if (far, side) == (0, 0):
        start = 2 * cut * second + chunk * size
        own_ref[:, :, start : start + size] = value
    elif not second:
        if far:
            y_ref[side, :, :, span] = value.astype(BF16)
        else:
            xa_ref[:, :, span] = value
    elif side:
        x_ref[far, :, :, span] = value.astype(BF16)
    else:
        yb_ref[:, :, span] = value


def out_grad(cut, where_ref, kind_ref, attnt_a, attnt_b, cot_a, cot_b, refs, left):
    g, c = where_ref[0], where_ref[2]
    count = attnt_a.shape[0]
    rows = left.shape[2] // 4
    half_width = cot_a.shape[2] // 2
    for far in range(2):
        kind = (g // 2) ^ far
        for i in range(2 * count):
            source = attnt_a if i < count else attnt_b
            keep = kind_ref[i] == kind
            for z in range(4):
                row = pl.multiple_of((2 * z + c) * rows, 16)
                value = source[i % count, pl.ds(row, rows), :]
                left[far, i // count, z * rows : (z + 1) * rows, (i % count) * LANES : (i % count + 1) * LANES] = (
                    jnp.where(keep, value, jnp.zeros_like(value))
                )
    for far in range(2):
        for side in range(2):
            column = ((g % 2) ^ side) * half_width
            for second, (at, size) in enumerate(((0, cut), (cut, half_width - cut))):
                span = pl.ds(pl.multiple_of(column + at, LANES), size)
                total = dot_nn(left[far, 0], cot_a[:, :, span].reshape(-1, size))
                total += dot_nn(left[far, 1], cot_b[:, :, span].reshape(-1, size))
                store(far, side, 0, second, total.reshape(4, rows, size), cut, refs)


def qkv_grad(cut, chunk, left, d_a, d_b, refs):
    rows = left.shape[2] // 8
    width = d_a.shape[2]
    for far in range(2):
        for second, (at, size) in enumerate(((0, cut), (cut, width - cut))):
            span = slice(at, at + size)
            total = dot_nn(left[far, 0], d_a[:, :, span].reshape(-1, size))
            total += dot_nn(left[far, 1], d_b[:, :, span].reshape(-1, size))
            total = total.reshape(2, 4, rows, size)
            for side in range(2):
                store(far, side, chunk, second, total[side], cut, refs)


def first_terms_kernel(cut, where_ref, kind_ref, left, attnt_a, attnt_b, cot_a, cot_b, dv_a, dv_b, *rest):
    refs, out_left = rest[:5], rest[5]
    out_grad(cut, where_ref, kind_ref, attnt_a, attnt_b, cot_a, cot_b, refs, out_left)
    qkv_grad(cut, 1, left, dv_a, dv_b, refs)


def second_terms_kernel(cut, left, dk_a, dk_b, dq_a, dq_b, *refs):
    qkv_grad(cut, 0, left, dk_a, dk_b, refs)
    qkv_grad(cut, 1, left, dq_a, dq_b, refs)


CUT = 384


def share_outputs(rows, width):
    first, second = 2 * CUT, 2 * (width - CUT)
    return [
        jax.ShapeDtypeStruct((2, 4, rows, first), BF16),
        jax.ShapeDtypeStruct((2, 4, rows, second), BF16),
        jax.ShapeDtypeStruct((4, rows, first + second), F32),
        jax.ShapeDtypeStruct((4, rows, first), F32),
        jax.ShapeDtypeStruct((4, rows, second), F32),
    ]


def left_factor(where, kinds, ht, ht_other):
    count, width, window = ht.shape
    return pl.pallas_call(
        left_kernel,
        out_shape=jax.ShapeDtypeStruct((2, 2, width // 2, count * window), BF16),
        in_specs=[SMEM, SMEM] + [VMEM] * 2,
        out_specs=VMEM,
        compiler_params=params(),
        cost_estimate=cost(0, 12 << 20),
        name="left_factor",
    )(where, kinds, ht, ht_other)


def first_terms(where, kinds, left, *pairs):
    count, inner, window = pairs[0].shape
    return pl.pallas_call(
        functools.partial(first_terms_kernel, CUT),
        out_shape=share_outputs(left.shape[2] // 8, inner),
        in_specs=[SMEM, SMEM] + [VMEM] * (1 + len(pairs)),
        out_specs=[VMEM] * 5,
        scratch_shapes=[pltpu.VMEM((2, 2, inner // 2, count * window), BF16)],
        compiler_params=params(),
        cost_estimate=cost(12 * count * window * left.shape[2] * inner, 12 << 20),
        name="first_terms",
    )(where, kinds, left, *pairs)


def second_terms(left, *pairs):
    count, window, inner = pairs[0].shape
    return pl.pallas_call(
        functools.partial(second_terms_kernel, CUT),
        out_shape=share_outputs(left.shape[2] // 8, inner),
        in_specs=[VMEM] * (1 + len(pairs)),
        out_specs=[VMEM] * 5,
        compiler_params=params(),
        cost_estimate=cost(16 * count * window * left.shape[2] * inner, 12 << 20),
        name="second_terms",
    )(left, *pairs)


def flat(groups, shards, move):
    pairs = []
    for g in range(groups):
        for d in range(shards):
            to_g, to_d = move(g, d)
            pairs.append((g * shards + d, to_g * shards + to_d))
    return pairs


def routes(groups, shards):
    chips = shards // 2
    make = functools.partial(flat, groups, shards)
    return {
        "sibling": make(lambda g, d: (g, d ^ 1)),
        "x": make(lambda g, d: (g ^ 1, d)),
        "y": make(lambda g, d: (g ^ 2, d)),
        "z": [
            make(lambda g, d, s=s: (g, (d // 2 + s) % chips * 2 + d % 2)) for s in range(chips)
        ],
    }


def send(value, route):
    return lax.ppermute(value, AXES, route)


def tied(value, *others):
    return lax.optimization_barrier((value, *others))[0]


def gather_weights(qkv_weight, out_weight, route, g, before_pass, before_last):
    kinds, rows, columns = qkv_weight.shape
    narrow = out_weight.shape[2] // 2
    quarters = jnp.concatenate(
        [
            qkv_weight.reshape(4, rows // 2, columns),
            out_weight.reshape(kinds, -1, 2, narrow).transpose(0, 2, 1, 3).reshape(4, -1, narrow),
        ],
        axis=2,
    )
    own = lax.dynamic_slice_in_dim(quarters, g, 1, 0)
    diagonal = lax.dynamic_slice_in_dim(quarters, g ^ 3, 1, 0)

    def in_plane(held):
        return send(held, route["x"]), send(held, route["y"])

    def pair(value):
        return [value, send(value, route["sibling"])]

    near = send(own, route["z"][1])
    pieces = pair(quarters)
    far = send(tied(near, before_pass), route["z"][1])
    near_x, near_y = in_plane(near)
    back = send(tied(own, near), route["z"][3])
    near_across = send(near_y, route["x"])
    pieces += pair(jnp.concatenate([near, near_x, near_y, near_across], axis=0))
    far_x, far_y = in_plane(far)
    back_across = send(tied(diagonal, far), route["z"][3])
    far_across = send(far_x, route["y"])
    back_x, back_y = in_plane(tied(back, before_last))
    pieces += pair(jnp.concatenate([far, far_x, far_y, far_across], axis=0))
    for piece in (back, back_x, back_y, back_across):
        pieces += pair(piece)
    return pieces


def reduce_plane(terms, route):
    to_y, to_x, own, x_term, y_term = terms
    from_y, from_x = send(to_y, route["y"]), send(to_x, route["x"])
    next_x = send((x_term + from_y[1].astype(F32)).astype(BF16), route["x"])
    next_y = send((y_term + from_x[1].astype(F32)).astype(BF16), route["y"])
    total = own + jnp.concatenate(
        [
            from_y[0].astype(F32) + next_x.astype(F32),
            from_x[0].astype(F32) + next_y.astype(F32),
        ],
        axis=-1,
    )
    return total, from_y


def reduce_line(total, route, z):
    mine = lax.dynamic_index_in_dim(total, z, 0, keepdims=False)
    for step in range(1, 4):
        part = lax.dynamic_index_in_dim(total, (z + step) % 4, 0, keepdims=False)
        mine += send(part.astype(BF16), route["z"][step]).astype(F32)
    return mine


def chunk_parts(share, inner):
    first, second = share[:, : 2 * CUT], share[:, 2 * CUT :]
    rest = inner - CUT
    return [
        jnp.concatenate([first[:, i * CUT : (i + 1) * CUT], second[:, i * rest : (i + 1) * rest]], axis=1)
        for i in range(2)
    ]


def whole_weights(qkv_weight, out_weight):
    return [
        lax.all_gather(qkv_weight, "dp", axis=1, tiled=True),
        lax.all_gather(out_weight, "dp", axis=1, tiled=True),
    ]


def summed_terms(kinds, h, dqkv, attn, cot):
    shards = lax.axis_size("dp")
    results = []
    for left, right in ((h, dqkv), (attn, cot)):
        parts = []
        for kind in range(2):
            keep = (kinds == kind)[:, None, None]
            parts.append(
                jnp.einsum("bwi,bwj->ij", jnp.where(keep, left, 0), right, preferred_element_type=F32)
            )
        total = lax.psum_scatter(
            jnp.stack(parts).reshape(2, shards, -1, right.shape[2]), "dp", scatter_dimension=1
        )
        total = lax.psum(total, "grp")
        results.append(lax.dynamic_index_in_dim(total, lax.axis_index("grp") // 2, 0, keepdims=False))
    return results


def shards(blocks, cotangent, modality, time_rank, qkv_weight, out_weight, norm_gain):
    groups, shard_count = lax.axis_size("grp"), lax.axis_size("dp")
    g, d = lax.axis_index("grp"), lax.axis_index("dp")
    z, c = d // 2, d % 2
    count, window, width = blocks.shape
    columns = qkv_weight.shape[2]
    inner = columns // 3
    routed = groups == 4 and shard_count == 8 and out_weight.shape[1] % 16 == 0
    where = jnp.stack([g, z, c]).astype(jnp.int32)
    gain = lax.all_gather(norm_gain, "dp", axis=1, tiled=True).astype(F32)

    rows = count * window
    h, ht = pl.pallas_call(
        norm_kernel,
        out_shape=[
            jax.ShapeDtypeStruct(blocks.shape, BF16),
            jax.ShapeDtypeStruct((count, width, window), BF16),
        ],
        in_specs=[SMEM, VMEM, VMEM],
        out_specs=[VMEM] * 2,
        compiler_params=params(),
        cost_estimate=cost(20 * rows * width, 8 * rows * width),
        name="norm",
    )(modality, blocks, gain)

    if routed:
        route = routes(groups, shard_count)
        kinds_other = send(modality.astype(F32), route["sibling"]).astype(jnp.int32)
        kinds = jnp.concatenate([modality, kinds_other])
        cot_other = send(cotangent, route["sibling"])
        ht_other = send(ht, route["sibling"])
        left = left_factor(where, kinds, ht, ht_other)
        weights = gather_weights(qkv_weight, out_weight, route, g, gain, ht_other)
        h = tied(h, left, cot_other)
    else:
        weights = whole_weights(qkv_weight, out_weight)
    n_weights = len(weights)
    weight_scratch = [
        pltpu.VMEM((2, width, columns), BF16),
        pltpu.VMEM((2, inner, width), BF16),
    ]
    weight_sems = pltpu.SemaphoreType.DMA((64,))

    attnt, dq, dk, dv = pl.pallas_call(
        functools.partial(layer_kernel, routed, n_weights),
        out_shape=[jax.ShapeDtypeStruct((count, inner, window), BF16)]
        + [jax.ShapeDtypeStruct((count, window, inner), BF16)] * 3,
        in_specs=[SMEM, SMEM, VMEM, VMEM] + [HBM] * n_weights,
        out_specs=[VMEM] * 4,
        scratch_shapes=weight_scratch
        + [pltpu.VMEM((window, columns), BF16), pltpu.VMEM((window, inner), BF16), weight_sems],
        compiler_params=params(),
        cost_estimate=cost(8 * rows * width * columns, 20 << 20),
        name="layer",
    )(where, modality, h, cotangent, *weights)

    result_attnt = attnt
    if routed:
        attnt_other, dv_other, dk_other, dq_other = [
            send(part, route["sibling"]) for part in (attnt, dv, dk, dq)
        ]
        first = first_terms(where, kinds, left, attnt, attnt_other, cotangent, cot_other, dv, dv_other)
        second = list(second_terms(left, tied(dk, first[0]), dk_other, dq, dq_other))
        result_attnt = tied(attnt, second[0])
        total, arrived = reduce_plane(first, route)
        second[0], second[1] = lax.optimization_barrier((second[0], second[1], arrived))[:2]
        shares = [reduce_line(total, route, z)]
        shares.append(reduce_line(reduce_plane(second, route)[0], route, z))
        parts = []
        for share in shares:
            other = send(share.astype(BF16), route["x"]).astype(F32)
            ordered = [jnp.where(g % 2 == i, share, other) for i in range(2)]
            parts += list(zip(*[chunk_parts(half, inner) for half in ordered]))
        out_halves, v_halves, k_halves, q_halves = parts
        share_out = jnp.concatenate(out_halves, axis=1)
        share_qkv = jnp.concatenate(
            [jnp.concatenate(halves, axis=0) for halves in (q_halves, k_halves, v_halves)], axis=1
        )
    else:
        share_qkv, share_out = summed_terms(
            modality, h, jnp.concatenate([dq, dk, dv], axis=2), attnt.transpose(0, 2, 1), cotangent
        )

    kind = g // 2
    own_weight = lax.dynamic_index_in_dim(qkv_weight, kind, 0, keepdims=False).astype(F32)
    own_gain = lax.dynamic_index_in_dim(norm_gain, kind, 0, keepdims=False).astype(F32)
    share_gain = jnp.sum(share_qkv * own_weight, axis=1) / own_gain

    encoded, block_grad = pl.pallas_call(
        functools.partial(result_kernel, routed, n_weights),
        out_shape=[jax.ShapeDtypeStruct(blocks.shape, BF16)] * 2,
        in_specs=[SMEM] * 3 + [VMEM] * 7 + [HBM] * n_weights,
        out_specs=[VMEM] * 2,
        scratch_shapes=weight_scratch + [pltpu.VMEM((window, width), F32), weight_sems],
        compiler_params=params(),
        cost_estimate=cost(2 * rows * width * (columns + inner), 20 << 20),
        name="result",
    )(where, modality, time_rank, blocks, cotangent, gain, result_attnt, dq, dk, dv, *weights)

    return (encoded, block_grad, share_qkv[None], share_out[None], share_gain[None])


def solution(mesh):
    return jax.shard_map(
        shards,
        mesh=mesh,
        in_specs=(
            P(("grp", "dp"), None, None),
            P(("grp", "dp"), None, None),
            P(("grp", "dp")),
            P(("grp", "dp")),
            P(None, "dp", None),
            P(None, "dp", None),
            P(None, "dp"),
        ),
        out_specs=(
            P(("grp", "dp"), None, None),
            P(("grp", "dp"), None, None),
            P("grp", "dp", None),
            P("grp", "dp", None),
            P("grp", "dp"),
        ),
        check_vma=False,
    )
```

```python
import functools
import math

import jax
import jax.numpy as jnp
from jax import lax
from jax.experimental import pallas as pl
from jax.experimental.pallas import tpu as pltpu
from jax.sharding import PartitionSpec as P

A_HEADS = 10
A_SIZE = 64
V_HEADS = 8
V_SIZE = 80
VWIN = 64
EPSILON = 1e-05
LANES = 128
AXES = ("grp", "dp")
VMEM_LIMIT = 60 * 1024 * 1024
BF16 = jnp.bfloat16
F32 = jnp.float32

VMEM = pl.BlockSpec(memory_space=pltpu.VMEM)
SMEM = pl.BlockSpec(memory_space=pltpu.SMEM)
HBM = pl.BlockSpec(memory_space=pl.ANY)


def params():
    return pltpu.CompilerParams(vmem_limit_bytes=VMEM_LIMIT)


def cost(microseconds):
    return pl.CostEstimate(flops=int(microseconds * 1.15e9), bytes_accessed=0, transcendentals=0)


def dot_nn(a, b):
    return lax.dot_general(a, b, (((1,), (0,)), ((), ())), preferred_element_type=F32)


def dot_nt(a, b):
    return lax.dot_general(a, b, (((1,), (1,)), ((), ())), preferred_element_type=F32)


def dot_tn(a, b):
    return lax.dot_general(a, b, (((0,), (0,)), ((), ())), preferred_element_type=F32)


def normalise(x):
    mean = jnp.mean(x, axis=-1, keepdims=True)
    centered = x - mean
    inverse = lax.rsqrt(jnp.mean(centered * centered, axis=-1, keepdims=True) + EPSILON)
    return centered * inverse, inverse


def norm_kernel(kind_ref, x_ref, gain_ref, h_ref, ht_ref):
    def body(b, carry):
        x_hat, _ = normalise(x_ref[b].astype(F32))
        h = (x_hat * gain_ref[pl.ds(kind_ref[b], 1), :]).astype(BF16)
        h_ref[b] = h
        ht_ref[b] = h.T
        return carry

    lax.fori_loop(0, x_ref.shape[0], body, 0)


def attend(b, heads, size, window, qkv, da, attnt_ref, dq_ref, dk_ref, dv_ref):
    rows = qkv.shape[0]
    inner = heads * size
    scale = 1.0 / math.sqrt(size)
    same = None
    if window < rows:
        key = lax.broadcasted_iota(jnp.int32, (rows, 2 * rows), 0) // window
        query = lax.broadcasted_iota(jnp.int32, (rows, 2 * rows), 1) % rows // window
        same = key == query
    sums = {}

    def add(name, tile, value):
        known = sums.get((name, tile))
        sums[name, tile] = value if known is None else known + value

    for head in range(0, heads, 2):
        first, last = head * size // LANES, ((head + 2) * size - 1) // LANES + 1
        low, wide = first * LANES, (last - first) * LANES
        lane = lax.broadcasted_iota(jnp.int32, (rows, wide), 1) + low
        row = lax.broadcasted_iota(jnp.int32, (wide, rows), 0) + low
        lanes = [(lane >= h * size) & (lane < (h + 1) * size) for h in (head, head + 1)]
        bands = [(row >= h * size) & (row < (h + 1) * size) for h in (head, head + 1)]
        q, k, v = (qkv[:, at + low : at + low + wide] for at in (0, inner, 2 * inner))
        g = da[:, low : low + wide]
        q_pair = jnp.concatenate([jnp.where(mask, q, 0) for mask in lanes], axis=0)
        g_pair = jnp.concatenate([jnp.where(mask, g, 0) for mask in lanes], axis=0)
        scores = dot_nt(k, q_pair) * scale
        if same is not None:
            scores = jnp.where(same, scores, -1e30)
        exponent = jnp.exp(scores - jnp.max(scores, axis=0, keepdims=True))
        probs = exponent * (1.0 / jnp.sum(exponent, axis=0, keepdims=True))
        d_probs = dot_nt(v, g_pair)
        mean = jnp.sum(d_probs * probs, axis=0, keepdims=True)
        d_scores = (probs * (d_probs - mean) * scale).astype(BF16)
        probs = probs.astype(BF16)
        d_v = dot_nn(probs, g_pair)
        d_k = dot_nn(d_scores, q_pair)
        vt, kt = v.T, k.T
        mixed = dot_nn(
            jnp.concatenate([jnp.where(band, vt, 0) for band in bands], axis=1),
            jnp.concatenate([probs[:, :rows], probs[:, rows:]], axis=0),
        )
        d_q = dot_nn(
            jnp.concatenate([jnp.where(band, kt, 0) for band in bands], axis=1),
            jnp.concatenate([d_scores[:, :rows], d_scores[:, rows:]], axis=0),
        )
        for tile in range(first, last):
            span = slice(tile * LANES - low, (tile + 1) * LANES - low)
            add("v", tile, d_v[:, span])
            add("k", tile, d_k[:, span])
            add("q", tile, d_q[span])
            add("o", tile, mixed[span])
        for tile in range(first, last):
            span = slice(tile * LANES, (tile + 1) * LANES)
            if (head + 2) * size >= (tile + 1) * LANES:
                dv_ref[b, :, span] = sums.pop(("v", tile)).astype(BF16)
                dk_ref[b, :, span] = sums.pop(("k", tile)).astype(BF16)
                dq_ref[b, :, span] = sums.pop(("q", tile)).astype(BF16).T
                attnt_ref[b, span, :] = sums.pop(("o", tile)).astype(BF16)


def routed_copies(where_ref, refs, wq, wo, sems):
    g, z, c = where_ref[0], where_ref[1], where_ref[2]
    half_rows, wide, narrow = refs[0].shape[1], wq.shape[2], wo.shape[2] // 2
    groups = [(2 + 8 * i + 2 * other, other, step) for i, step in enumerate((3, 2, 1)) for other in range(4)]
    by_kind = []
    for far in range(2):
        kind = (g // 2) ^ far
        first, second = [], []
        for side in range(2):
            half = (g % 2) ^ side
            found = [(refs[i], 2 * kind + half, 2 * z + core) for i, core in ((0, c), (1, 1 - c))]
            for i, other, step in groups:
                if other == 2 * far + side:
                    chip = 2 * lax.rem(z + step, 4)
                    found += [(refs[i], 0, chip + c), (refs[i + 1], 0, chip + 1 - c)]
            for ref, at, shard in found:
                row = pl.multiple_of((shard * 2 + half) * half_rows, 16)
                out_row = pl.multiple_of(shard * half_rows, 16)
                column = pl.multiple_of(half * narrow, LANES)
                first.append(
                    pltpu.make_async_copy(
                        ref.at[at, :, pl.ds(0, wide)],
                        wq.at[kind, pl.ds(row, half_rows), :],
                        sems.at[far, len(first)],
                    )
                )
                second.append(
                    pltpu.make_async_copy(
                        ref.at[at, :, pl.ds(wide, narrow)],
                        wo.at[kind, pl.ds(out_row, half_rows), pl.ds(column, narrow)],
                        sems.at[far, 16 + len(second)],
                    )
                )
        by_kind.append(first + second)
    return by_kind


def weight_copies(routed, where_ref, refs, wq, wo, sems):
    if routed:
        return routed_copies(where_ref, refs, wq, wo, sems)
    return [
        [
            pltpu.make_async_copy(ref.at[kind], to.at[kind], sems.at[kind, i])
            for i, (ref, to) in enumerate(zip(refs, (wq, wo)))
        ]
        for kind in range(2)
    ]


def by_encoder(routed, where_ref, kind_ref, copies, body):
    for group in copies:
        for copy in group:
            copy.start()
    blocks = kind_ref.shape[0]
    first = where_ref[0] // 2 if routed else 0

    def step(i, carry):
        b, far = lax.rem(i, blocks), lax.div(i, blocks)
        for turn, group in enumerate(copies):

            @pl.when(i == turn * blocks)
            def _():
                for copy in group:
                    copy.wait()

        kind = first ^ far

        @pl.when(kind_ref[b] == kind)
        def _():
            body(b, kind)

        return carry

    lax.fori_loop(0, 2 * blocks, step, 0)


def layer_kernel(routed, n_weights, where_ref, kind_ref, h_ref, cot_ref, *rest):
    weights, rest = rest[:n_weights], rest[n_weights:]
    attnt_ref, dq_ref, dk_ref, dv_ref, wq, wo, qkv_ref, da_ref, sems = rest
    chunk = 3 * LANES

    def body(b, kind):
        for at in range(0, wq.shape[2], chunk):
            qkv_ref[:, at : at + chunk] = dot_nn(h_ref[b], wq[kind, :, at : at + chunk]).astype(BF16)
        for at in range(0, wo.shape[1], LANES):
            da_ref[:, at : at + LANES] = dot_nt(cot_ref[b], wo[kind, at : at + LANES, :]).astype(BF16)

        @pl.when(kind == 0)
        def _():
            attend(b, A_HEADS, A_SIZE, qkv_ref.shape[0], qkv_ref, da_ref, attnt_ref, dq_ref, dk_ref, dv_ref)

        @pl.when(kind != 0)
        def _():
            attend(b, V_HEADS, V_SIZE, VWIN, qkv_ref, da_ref, attnt_ref, dq_ref, dk_ref, dv_ref)

    by_encoder(routed, where_ref, kind_ref, weight_copies(routed, where_ref, weights, wq, wo, sems), body)


def result_kernel(routed, n_weights, where_ref, kind_ref, rank_ref, x_ref, cot_ref, gain_ref, attnt_ref, dq_ref, dk_ref, dv_ref, *rest):
    weights, rest = rest[:n_weights], rest[n_weights:]
    encoded_ref, grad_ref, wq, wo, wide_ref, sems = rest
    inner = dq_ref.shape[2]
    chunk = 2 * LANES
    width = x_ref.shape[2]

    def body(b, kind):
        rank = rank_ref[b]
        attn = attnt_ref[b].T
        for at in range(0, width, chunk):
            span = slice(at, at + chunk)
            encoded_ref[rank, :, span] = (
                x_ref[b, :, span].astype(F32) + dot_nn(attn, wo[kind, :, span])
            ).astype(BF16)
            wide_ref[:, span] = (
                dot_nt(dq_ref[b], wq[kind, span, :inner])
                + dot_nt(dk_ref[b], wq[kind, span, inner : 2 * inner])
                + dot_nt(dv_ref[b], wq[kind, span, 2 * inner :])
            )
        x_hat, inverse = normalise(x_ref[b].astype(F32))
        scaled = wide_ref[...] * gain_ref[pl.ds(kind, 1), :]
        d_input = inverse * (
            scaled
            - jnp.mean(scaled, axis=-1, keepdims=True)
            - x_hat * jnp.mean(scaled * x_hat, axis=-1, keepdims=True)
        )
        grad_ref[rank] = (cot_ref[b].astype(F32) + d_input).astype(BF16)

    by_encoder(routed, where_ref, kind_ref, weight_copies(routed, where_ref, weights, wq, wo, sems), body)


def left_kernel(where_ref, kind_ref, ht_a, ht_b, left):
    g, c = where_ref[0], where_ref[2]
    count = ht_a.shape[0]
    rows = left.shape[2] // 8
    for far in range(2):
        kind = (g // 2) ^ far
        for i in range(2 * count):
            source = ht_a if i < count else ht_b
            keep = kind_ref[i] == kind
            for side in range(2):
                for z in range(4):
                    row = pl.multiple_of(((2 * z + c) * 2 + ((g % 2) ^ side)) * rows, 16)
                    value = source[i % count, pl.ds(row, rows), :]
                    at = (side * 4 + z) * rows
                    left[far, i // count, at : at + rows, (i % count) * LANES : (i % count + 1) * LANES] = (
                        jnp.where(keep, value, jnp.zeros_like(value))
                    )


def out_terms_kernel(where_ref, kind_ref, attnt_a, attnt_b, cot_a, cot_b, own_ref, far_ref, sent_ref, left):
    g, z, c = where_ref[0], where_ref[1], where_ref[2]
    count = attnt_a.shape[0]
    rows = left.shape[2] // 4
    half_width = cot_a.shape[2] // 2
    for far in range(2):
        kind = (g // 2) ^ far
        for i in range(2 * count):
            source = attnt_a if i < count else attnt_b
            keep = kind_ref[i] == kind
            for step in range(4):
                row = pl.multiple_of((2 * (z ^ step) + c) * rows, 16)
                value = source[i % count, pl.ds(row, rows), :]
                left[far, i // count, step * rows : (step + 1) * rows, (i % count) * LANES : (i % count + 1) * LANES] = (
                    jnp.where(keep, value, jnp.zeros_like(value))
                )
    for far in range(2):
        for side in range(2):
            span = pl.ds(pl.multiple_of(((g % 2) ^ side) * half_width, LANES), half_width)
            total = dot_nn(left[far, 0], cot_a[:, :, span].reshape(-1, half_width))
            total += dot_nn(left[far, 1], cot_b[:, :, span].reshape(-1, half_width))
            total = total.reshape(4, rows, half_width)
            own_ref[2 * far + side] = total[0]
            far_ref[2 * far + side] = total[2]
            sent_ref[0, 2 * far + side] = total[1].astype(BF16)
            sent_ref[1, 2 * far + side] = total[3].astype(BF16)


def qkv_terms_kernel(left, *rest):
    pairs, (y_ref, x_ref, own_ref, xa_ref, yb_ref) = rest[:6], rest[6:]
    rows = left.shape[2] // 8
    width, cut = pairs[0].shape[2], xa_ref.shape[2]
    chunk = 3 * LANES
    for far in range(2):
        for part in range(3):
            d_a, d_b = pairs[2 * part : 2 * part + 2]
            for low in range(0, width, chunk):
                size = min(chunk, width - low)
                span = slice(low, low + size)
                total = dot_nn(left[far, 0], d_a[:, :, span].reshape(-1, size))
                total += dot_nn(left[far, 1], d_b[:, :, span].reshape(-1, size))
                total = total.reshape(2, 4, rows, size)
                at = part * width + low
                first = slice(at, at + size)
                last = slice(at - cut, at - cut + size)
                if far == 0:
                    own_ref[:, :, first] = total[0]
                for side in range(2):
                    if (far, side) == (0, 0):
                        continue
                    if at < cut and far:
                        y_ref[side, :, :, first] = total[side].astype(BF16)
                    elif at < cut:
                        xa_ref[:, :, first] = total[side]
                    elif side:
                        x_ref[far, :, :, last] = total[side].astype(BF16)
                    else:
                        yb_ref[:, :, last] = total[side]


QKV_CUT = 1024
STEPS = ((slice(0, 512), slice(0, 512)), (slice(512, None), slice(512, None)))
OUT_CUT = 384


def left_factor(where, kinds, ht, ht_other):
    count, width, window = ht.shape
    return pl.pallas_call(
        left_kernel,
        out_shape=jax.ShapeDtypeStruct((2, 2, width // 2, count * window), BF16),
        in_specs=[SMEM, SMEM] + [VMEM] * 2,
        out_specs=VMEM,
        compiler_params=params(),
        cost_estimate=cost(0.01),
        name="left_factor",
    )(where, kinds, ht, ht_other)


def out_terms(where, kinds, *pairs):
    count, inner, window = pairs[0].shape
    rows, width = inner // 8, pairs[2].shape[2] // 2
    return pl.pallas_call(
        out_terms_kernel,
        out_shape=[
            jax.ShapeDtypeStruct((4, rows, width), F32),
            jax.ShapeDtypeStruct((4, rows, width), F32),
            jax.ShapeDtypeStruct((2, 4, rows, width), BF16),
        ],
        in_specs=[SMEM, SMEM] + [VMEM] * len(pairs),
        out_specs=[VMEM] * 3,
        scratch_shapes=[pltpu.VMEM((2, 2, inner // 2, count * window), BF16)],
        compiler_params=params(),
        cost_estimate=cost(0.01),
        name="out_terms",
    )(where, kinds, *pairs)


def qkv_terms(left, *pairs):
    rows, columns = left.shape[2] // 8, 3 * pairs[0].shape[2]
    rest = columns - QKV_CUT
    return pl.pallas_call(
        qkv_terms_kernel,
        out_shape=[
            jax.ShapeDtypeStruct((2, 4, rows, QKV_CUT), BF16),
            jax.ShapeDtypeStruct((2, 4, rows, rest), BF16),
            jax.ShapeDtypeStruct((4, rows, columns), F32),
            jax.ShapeDtypeStruct((4, rows, QKV_CUT), F32),
            jax.ShapeDtypeStruct((4, rows, rest), F32),
        ],
        in_specs=[VMEM] * (1 + len(pairs)),
        out_specs=[VMEM] * 5,
        compiler_params=params(),
        cost_estimate=cost(0.01),
        name="qkv_terms",
    )(left, *pairs)


def flat(groups, shards, move):
    pairs = []
    for g in range(groups):
        for d in range(shards):
            to_g, to_d = move(g, d)
            pairs.append((g * shards + d, to_g * shards + to_d))
    return pairs


def routes(groups, shards):
    chips = shards // 2
    make = functools.partial(flat, groups, shards)
    return {
        "sibling": make(lambda g, d: (g, d ^ 1)),
        "x": make(lambda g, d: (g ^ 1, d)),
        "y": make(lambda g, d: (g ^ 2, d)),
        "z1": make(lambda g, d: (g, d ^ 2)),
        "z2": make(lambda g, d: (g, d ^ 4)),
        "z": [
            make(lambda g, d, s=s: (g, (d // 2 + s) % chips * 2 + d % 2)) for s in range(chips)
        ],
    }


def send(value, route):
    return lax.ppermute(value, AXES, route)


def tied(value, *others):
    return lax.optimization_barrier((value, *others))[0]


def gather_small(norm_gain, modality, route, z, c):
    kinds, rows = norm_gain.shape
    gains = norm_gain.astype(F32).reshape(1, -1)
    sibling = send(jnp.concatenate([gains, modality.astype(F32)[None]], axis=1), route["sibling"])
    others, kinds_other = sibling[:, : kinds * rows], sibling[0, kinds * rows :].astype(jnp.int32)
    pair = jnp.concatenate([jnp.where(c == 0, gains, others), jnp.where(c == 0, others, gains)], axis=0)
    chips = jnp.arange(4)[:, None, None]
    total = jnp.where(chips == z, pair[None], 0)
    for step in range(1, 4):
        total += jnp.where(chips == (z + 4 - step) % 4, send(pair, route["z"][step])[None], 0)
    return total.reshape(8, kinds, rows).transpose(1, 0, 2).reshape(kinds, -1), kinds_other


def quarter_of(qkv_weight, out_weight, q):
    rows, narrow = qkv_weight.shape[1] // 2, out_weight.shape[2] // 2
    own_qkv = lax.dynamic_slice(qkv_weight, (q // 2, q % 2 * rows, 0), (1, rows, qkv_weight.shape[2]))
    own_out = lax.dynamic_slice(out_weight, (q // 2, 0, q % 2 * narrow), (1, out_weight.shape[1], narrow))
    return jnp.concatenate([own_qkv, own_out], axis=2)


def quarters_of(qkv_weight, out_weight):
    kinds, rows, columns = qkv_weight.shape
    narrow = out_weight.shape[2] // 2
    return jnp.concatenate(
        [
            qkv_weight.reshape(4, rows // 2, columns),
            out_weight.reshape(kinds, -1, 2, narrow).transpose(0, 2, 1, 3).reshape(4, -1, narrow),
        ],
        axis=2,
    )


def send_terms(terms, route):
    to_y, to_x = terms[:2]
    return send(to_y, route["y"]), send(to_x, route["x"])


def reduce_plane(terms, arrived, route):
    _, _, own, x_term, y_term = terms
    from_y, from_x = arrived
    next_x = send((x_term + from_y[1].astype(F32)).astype(BF16), route["x"])
    next_y = send((y_term + from_x[1].astype(F32)).astype(BF16), route["y"])
    return own + jnp.concatenate(
        [
            from_y[0].astype(F32) + next_x.astype(F32),
            from_x[0].astype(F32) + next_y.astype(F32),
        ],
        axis=-1,
    )


def line_parts(total, z):
    parts = [lax.dynamic_index_in_dim(total, (z + step) % 4, 0, keepdims=False) for step in range(4)]
    return [parts[0]] + [part.astype(BF16) for part in parts[1:]]


def send_line(parts, route):
    return [send(parts[step], route["z"][step]) for step in range(1, 4)]


def add_line(own, arrived):
    return own + sum(part.astype(F32) for part in arrived)


def plane_terms(total, cut):
    first, second = total[..., :cut], total[..., cut:]
    return [
        first[2:].astype(BF16),
        jnp.stack([second[1], second[3]]).astype(BF16),
        total[0],
        first[1],
        second[2],
    ]


def both_halves(share, g, route):
    other = send(share.astype(BF16), route["x"]).astype(F32)
    return [jnp.where(g % 2 == i, share, other) for i in range(2)]


def whole_weights(qkv_weight, out_weight):
    return [
        lax.all_gather(qkv_weight, "dp", axis=1, tiled=True),
        lax.all_gather(out_weight, "dp", axis=1, tiled=True),
    ]


def summed_terms(kinds, h, dqkv, attn, cot):
    shards = lax.axis_size("dp")
    results = []
    for left, right in ((h, dqkv), (attn, cot)):
        parts = []
        for kind in range(2):
            keep = (kinds == kind)[:, None, None]
            parts.append(
                jnp.einsum("bwi,bwj->ij", jnp.where(keep, left, 0), right, preferred_element_type=F32)
            )
        total = lax.psum_scatter(
            jnp.stack(parts).reshape(2, shards, -1, right.shape[2]), "dp", scatter_dimension=1
        )
        total = lax.psum(total, "grp")
        results.append(lax.dynamic_index_in_dim(total, lax.axis_index("grp") // 2, 0, keepdims=False))
    return results


def shards(blocks, cotangent, modality, time_rank, qkv_weight, out_weight, norm_gain):
    groups, shard_count = lax.axis_size("grp"), lax.axis_size("dp")
    g, d = lax.axis_index("grp"), lax.axis_index("dp")
    z, c = d // 2, d % 2
    count, window, width = blocks.shape
    columns = qkv_weight.shape[2]
    inner = columns // 3
    routed = groups == 4 and shard_count == 8 and out_weight.shape[1] % 16 == 0
    where = jnp.stack([g, z, c]).astype(jnp.int32)
    rows = count * window

    def normed(blocks, gain):
        return pl.pallas_call(
            norm_kernel,
            out_shape=[
                jax.ShapeDtypeStruct(blocks.shape, BF16),
                jax.ShapeDtypeStruct((count, width, window), BF16),
            ],
            in_specs=[SMEM, VMEM, VMEM],
            out_specs=[VMEM] * 2,
            compiler_params=params(),
            cost_estimate=cost(0.01),
            name="norm",
        )(modality, blocks, gain)

    if routed:
        route = routes(groups, shard_count)

        def in_plane(held):
            return send(held, route["x"]), send(held, route["y"])

        def sibling(value, *after):
            return send(tied(value, *after) if after else value, route["sibling"])

        own = quarter_of(qkv_weight, out_weight, g)
        near = send(own, route["z"][1])
        gain, kinds_other = gather_small(tied(norm_gain, own), modality, route, z, c)
        near = tied(near, gain)
        far = send(near, route["z"][1])
        near_x, near_y = in_plane(near)
        h, ht = normed(tied(blocks, near), gain)
        quarters = quarters_of(tied(qkv_weight, near), out_weight)
        diagonal = lax.dynamic_slice_in_dim(quarters, g ^ 3, 1, 0)
        quarters_other = sibling(quarters)
        cot_other = sibling(cotangent, near)
        far = tied(far, near_x, near_y, h, quarters_other)
        far_x, far_y = in_plane(far)
        back = send(tied(own, far), route["z"][3])
        kinds = jnp.concatenate([modality, kinds_other])
        ht_other = sibling(ht, far)
        left = left_factor(where, kinds, ht, ht_other)
        near_other = sibling(near, far)
        near_x_other = sibling(near_x, near_other)
        near_y_other = sibling(near_y, near_other)
        back = tied(back, far_x, far_y, left, near_other)
        back_x, back_y = in_plane(back)
        near_across = send(tied(diagonal, back), route["z"][1])
        far_other = sibling(far, back)
        far_x_other = sibling(far_x, far_other)
        far_y_other = sibling(far_y, far_other)
        back_other = sibling(back, far_other)
        far_across = send(tied(far_x, back_x, back_y), route["y"])
        back_across = send(tied(diagonal, near_across), route["z"][3])
        weights = [quarters, quarters_other, near, near_other, near_x, near_x_other, near_y, near_y_other]
        weights += [near_across, sibling(near_across), far, far_other, far_x, far_x_other, far_y, far_y_other]
        weights += [far_across, sibling(far_across), back, back_other, back_x, sibling(back_x)]
        weights += [back_y, sibling(back_y), back_across, sibling(back_across)]
    else:
        gain = lax.all_gather(norm_gain, "dp", axis=1, tiled=True).astype(F32)
        weights = whole_weights(qkv_weight, out_weight)
        h, ht = normed(blocks, gain)
    n_weights = len(weights)
    weight_scratch = [
        pltpu.VMEM((2, width, columns), BF16),
        pltpu.VMEM((2, inner, width), BF16),
    ]
    weight_sems = pltpu.SemaphoreType.DMA((2, 32))

    attnt, dq, dk, dv = pl.pallas_call(
        functools.partial(layer_kernel, routed, n_weights),
        out_shape=[jax.ShapeDtypeStruct((count, inner, window), BF16)]
        + [jax.ShapeDtypeStruct((count, window, inner), BF16)] * 3,
        in_specs=[SMEM, SMEM, VMEM, VMEM] + [HBM] * n_weights,
        out_specs=[VMEM] * 4,
        scratch_shapes=weight_scratch
        + [pltpu.VMEM((window, columns), BF16), pltpu.VMEM((window, inner), BF16), weight_sems],
        compiler_params=params(),
        cost_estimate=cost(0.01),
        name="layer",
    )(where, modality, h, cotangent, *weights)

    def results(attnt):
        return pl.pallas_call(
            functools.partial(result_kernel, routed, n_weights),
            out_shape=[jax.ShapeDtypeStruct(blocks.shape, BF16)] * 2,
            in_specs=[SMEM] * 3 + [VMEM] * 7 + [HBM] * n_weights,
            out_specs=[VMEM] * 2,
            scratch_shapes=weight_scratch + [pltpu.VMEM((window, width), F32), weight_sems],
            compiler_params=params(),
            cost_estimate=cost(0.01),
            name="result",
        )(where, modality, time_rank, blocks, cotangent, gain, attnt, dq, dk, dv, *weights)

    if routed:
        dq_other, dk_other, dv_other, attnt_other = [
            send(part, route["sibling"]) for part in (dq, dk, dv, attnt)
        ]
        terms = qkv_terms(left, dq, dq_other, dk, dk_other, dv, dv_other)
        arrived = send_terms(terms, route)
        out_own, out_far, out_sent = out_terms(
            where, kinds, tied(attnt, terms[0]), attnt_other, cotangent, cot_other
        )
        out_near = send(out_sent, route["z1"])
        encoded, block_grad = results(tied(attnt, out_own))
        out_near, *arrived = lax.optimization_barrier((out_near, *arrived, encoded))[:3]
        parts = []
        for first, last in STEPS:
            step_arrived = (arrived[0][..., first], arrived[1][..., last])
            own = jnp.concatenate([terms[2][..., :QKV_CUT][..., first], terms[2][..., QKV_CUT:][..., last]], axis=2)
            step_terms = (None, None, own, terms[3][..., first], terms[4][..., last])
            parts.append(line_parts(reduce_plane(step_terms, step_arrived, route), z))
        out_next = send((out_far + out_near[1].astype(F32)).astype(BF16), route["z2"])
        shares = [add_line(part[0], send_line(part, route)) for part in parts]
        out_total = tied(out_own + out_near[0].astype(F32) + out_next.astype(F32), *parts[1])
        terms = plane_terms(out_total, OUT_CUT)
        share = reduce_plane(terms, send_terms(terms, route), route)
        share_out = jnp.concatenate(both_halves(share, g, route), axis=1)
        (first_a, first_b), (last_a, last_b) = [
            tuple(zip(*[(half[:, :512], half[:, 512:]) for half in both_halves(share, g, route)]))
            for share in shares
        ]
        share_qkv = jnp.concatenate(
            [jnp.concatenate(halves, axis=0) for halves in (first_a, last_a, first_b, last_b)], axis=1
        )
    else:
        encoded, block_grad = results(attnt)
        share_qkv, share_out = summed_terms(
            modality, h, jnp.concatenate([dq, dk, dv], axis=2), attnt.transpose(0, 2, 1), cotangent
        )

    kind = g // 2
    own_weight = lax.dynamic_index_in_dim(qkv_weight, kind, 0, keepdims=False).astype(F32)
    own_gain = lax.dynamic_index_in_dim(norm_gain, kind, 0, keepdims=False).astype(F32)
    share_gain = jnp.sum(share_qkv * own_weight, axis=1) / own_gain

    return (encoded, block_grad, share_qkv[None], share_out[None], share_gain[None])


def solution(mesh):
    return jax.shard_map(
        shards,
        mesh=mesh,
        in_specs=(
            P(("grp", "dp"), None, None),
            P(("grp", "dp"), None, None),
            P(("grp", "dp")),
            P(("grp", "dp")),
            P(None, "dp", None),
            P(None, "dp", None),
            P(None, "dp"),
        ),
        out_specs=(
            P(("grp", "dp"), None, None),
            P(("grp", "dp"), None, None),
            P("grp", "dp", None),
            P("grp", "dp", None),
            P("grp", "dp"),
        ),
        check_vma=False,
    )
```

```python
import functools
import math

import jax
import jax.numpy as jnp
from jax import lax
from jax.experimental import pallas as pl
from jax.experimental.pallas import tpu as pltpu
from jax.sharding import PartitionSpec as P

A_HEADS = 10
A_SIZE = 64
V_HEADS = 8
V_SIZE = 80
VWIN = 64
EPSILON = 1e-05
LANES = 128
AXES = ("grp", "dp")
VMEM_LIMIT = 60 * 1024 * 1024
BF16 = jnp.bfloat16
F32 = jnp.float32

VMEM = pl.BlockSpec(memory_space=pltpu.VMEM)
SMEM = pl.BlockSpec(memory_space=pltpu.SMEM)
HBM = pl.BlockSpec(memory_space=pl.ANY)


def params():
    return pltpu.CompilerParams(vmem_limit_bytes=VMEM_LIMIT)


def cost(microseconds):
    return pl.CostEstimate(flops=int(microseconds * 1.15e9), bytes_accessed=0, transcendentals=0)


def dot_nn(a, b):
    return lax.dot_general(a, b, (((1,), (0,)), ((), ())), preferred_element_type=F32)


def dot_nt(a, b):
    return lax.dot_general(a, b, (((1,), (1,)), ((), ())), preferred_element_type=F32)


def dot_tn(a, b):
    return lax.dot_general(a, b, (((0,), (0,)), ((), ())), preferred_element_type=F32)


def normalise(x):
    mean = jnp.mean(x, axis=-1, keepdims=True)
    centered = x - mean
    inverse = lax.rsqrt(jnp.mean(centered * centered, axis=-1, keepdims=True) + EPSILON)
    return centered * inverse, inverse


def norm_kernel(kind_ref, x_ref, gain_ref, h_ref, ht_ref):
    def body(b, carry):
        x_hat, _ = normalise(x_ref[b].astype(F32))
        h = (x_hat * gain_ref[pl.ds(kind_ref[b], 1), :]).astype(BF16)
        h_ref[b] = h
        ht_ref[b] = h.T
        return carry

    lax.fori_loop(0, x_ref.shape[0], body, 0)


def attend(b, heads, size, window, qkv, da, attnt_ref, dq_ref, dk_ref, dv_ref):
    rows = qkv.shape[0]
    inner = heads * size
    scale = 1.0 / math.sqrt(size)
    same = None
    if window < rows:
        key = lax.broadcasted_iota(jnp.int32, (rows, 2 * rows), 0) // window
        query = lax.broadcasted_iota(jnp.int32, (rows, 2 * rows), 1) % rows // window
        same = key == query
    sums = {}

    def add(name, tile, value):
        known = sums.get((name, tile))
        sums[name, tile] = value if known is None else known + value

    for head in range(0, heads, 2):
        first, last = head * size // LANES, ((head + 2) * size - 1) // LANES + 1
        low, wide = first * LANES, (last - first) * LANES
        lane = lax.broadcasted_iota(jnp.int32, (rows, wide), 1) + low
        row = lax.broadcasted_iota(jnp.int32, (wide, rows), 0) + low
        lanes = [(lane >= h * size) & (lane < (h + 1) * size) for h in (head, head + 1)]
        bands = [(row >= h * size) & (row < (h + 1) * size) for h in (head, head + 1)]
        q, k, v = (qkv[:, at + low : at + low + wide] for at in (0, inner, 2 * inner))
        g = da[:, low : low + wide]
        q_pair = jnp.concatenate([jnp.where(mask, q, 0) for mask in lanes], axis=0)
        g_pair = jnp.concatenate([jnp.where(mask, g, 0) for mask in lanes], axis=0)
        scores = dot_nt(k, q_pair) * scale
        if same is not None:
            scores = jnp.where(same, scores, -1e30)
        exponent = jnp.exp(scores - jnp.max(scores, axis=0, keepdims=True))
        probs = exponent * (1.0 / jnp.sum(exponent, axis=0, keepdims=True))
        d_probs = dot_nt(v, g_pair)
        mean = jnp.sum(d_probs * probs, axis=0, keepdims=True)
        d_scores = (probs * (d_probs - mean) * scale).astype(BF16)
        probs = probs.astype(BF16)
        d_v = dot_nn(probs, g_pair)
        d_k = dot_nn(d_scores, q_pair)
        vt, kt = v.T, k.T
        mixed = dot_nn(
            jnp.concatenate([jnp.where(band, vt, 0) for band in bands], axis=1),
            jnp.concatenate([probs[:, :rows], probs[:, rows:]], axis=0),
        )
        d_q = dot_nn(
            jnp.concatenate([jnp.where(band, kt, 0) for band in bands], axis=1),
            jnp.concatenate([d_scores[:, :rows], d_scores[:, rows:]], axis=0),
        )
        for tile in range(first, last):
            span = slice(tile * LANES - low, (tile + 1) * LANES - low)
            add("v", tile, d_v[:, span])
            add("k", tile, d_k[:, span])
            add("q", tile, d_q[span])
            add("o", tile, mixed[span])
        for tile in range(first, last):
            span = slice(tile * LANES, (tile + 1) * LANES)
            if (head + 2) * size >= (tile + 1) * LANES:
                dv_ref[b, :, span] = sums.pop(("v", tile)).astype(BF16)
                dk_ref[b, :, span] = sums.pop(("k", tile)).astype(BF16)
                dq_ref[b, :, span] = sums.pop(("q", tile)).astype(BF16).T
                attnt_ref[b, span, :] = sums.pop(("o", tile)).astype(BF16)


def routed_copies(where_ref, refs, wq, wo, sems):
    g, z, c = where_ref[0], where_ref[1], where_ref[2]
    half_rows, wide, narrow = refs[0].shape[1], wq.shape[2], wo.shape[2] // 2
    groups = [(2 + 8 * i + 2 * other, other, step) for i, step in enumerate((3, 2, 1)) for other in range(4)]
    by_kind = []
    for far in range(2):
        kind = (g // 2) ^ far
        first, second = [], []
        for side in range(2):
            half = (g % 2) ^ side
            found = [(refs[i], 2 * kind + half, 2 * z + core) for i, core in ((0, c), (1, 1 - c))]
            for i, other, step in groups:
                if other == 2 * far + side:
                    chip = 2 * lax.rem(z + step, 4)
                    found += [(refs[i], 0, chip + c), (refs[i + 1], 0, chip + 1 - c)]
            for ref, at, shard in found:
                row = pl.multiple_of((shard * 2 + half) * half_rows, 16)
                out_row = pl.multiple_of(shard * half_rows, 16)
                column = pl.multiple_of(half * narrow, LANES)
                first.append(
                    pltpu.make_async_copy(
                        ref.at[at, :, pl.ds(0, wide)],
                        wq.at[kind, pl.ds(row, half_rows), :],
                        sems.at[far, len(first)],
                    )
                )
                second.append(
                    pltpu.make_async_copy(
                        ref.at[at, :, pl.ds(wide, narrow)],
                        wo.at[kind, pl.ds(out_row, half_rows), pl.ds(column, narrow)],
                        sems.at[far, 16 + len(second)],
                    )
                )
        by_kind.append(first + second)
    return by_kind


def weight_copies(routed, where_ref, refs, wq, wo, sems):
    if routed:
        return routed_copies(where_ref, refs, wq, wo, sems)
    return [
        [
            pltpu.make_async_copy(ref.at[kind], to.at[kind], sems.at[kind, i])
            for i, (ref, to) in enumerate(zip(refs, (wq, wo)))
        ]
        for kind in range(2)
    ]


def by_encoder(routed, where_ref, kind_ref, copies, body):
    for group in copies:
        for copy in group:
            copy.start()
    blocks = kind_ref.shape[0]
    first = where_ref[0] // 2 if routed else 0

    def step(i, carry):
        b, far = lax.rem(i, blocks), lax.div(i, blocks)
        for turn, group in enumerate(copies):

            @pl.when(i == turn * blocks)
            def _():
                for copy in group:
                    copy.wait()

        kind = first ^ far

        @pl.when(kind_ref[b] == kind)
        def _():
            body(b, kind)

        return carry

    lax.fori_loop(0, 2 * blocks, step, 0)


def layer_kernel(routed, n_weights, where_ref, kind_ref, h_ref, cot_ref, *rest):
    weights, rest = rest[:n_weights], rest[n_weights:]
    attnt_ref, dq_ref, dk_ref, dv_ref, wq, wo, qkv_ref, da_ref, sems = rest
    chunk = 3 * LANES

    def body(b, kind):
        for at in range(0, wq.shape[2], chunk):
            qkv_ref[:, at : at + chunk] = dot_nn(h_ref[b], wq[kind, :, at : at + chunk]).astype(BF16)
        for at in range(0, wo.shape[1], LANES):
            da_ref[:, at : at + LANES] = dot_nt(cot_ref[b], wo[kind, at : at + LANES, :]).astype(BF16)

        @pl.when(kind == 0)
        def _():
            attend(b, A_HEADS, A_SIZE, qkv_ref.shape[0], qkv_ref, da_ref, attnt_ref, dq_ref, dk_ref, dv_ref)

        @pl.when(kind != 0)
        def _():
            attend(b, V_HEADS, V_SIZE, VWIN, qkv_ref, da_ref, attnt_ref, dq_ref, dk_ref, dv_ref)

    by_encoder(routed, where_ref, kind_ref, weight_copies(routed, where_ref, weights, wq, wo, sems), body)


def result_kernel(routed, n_weights, where_ref, kind_ref, rank_ref, x_ref, cot_ref, gain_ref, attnt_ref, dq_ref, dk_ref, dv_ref, *rest):
    weights, rest = rest[:n_weights], rest[n_weights:]
    encoded_ref, grad_ref, wq, wo, wide_ref, sems = rest
    inner = dq_ref.shape[2]
    chunk = 2 * LANES
    width = x_ref.shape[2]

    def body(b, kind):
        rank = rank_ref[b]
        attn = attnt_ref[b].T
        for at in range(0, width, chunk):
            span = slice(at, at + chunk)
            encoded_ref[rank, :, span] = (
                x_ref[b, :, span].astype(F32) + dot_nn(attn, wo[kind, :, span])
            ).astype(BF16)
            wide_ref[:, span] = (
                dot_nt(dq_ref[b], wq[kind, span, :inner])
                + dot_nt(dk_ref[b], wq[kind, span, inner : 2 * inner])
                + dot_nt(dv_ref[b], wq[kind, span, 2 * inner :])
            )
        x_hat, inverse = normalise(x_ref[b].astype(F32))
        scaled = wide_ref[...] * gain_ref[pl.ds(kind, 1), :]
        d_input = inverse * (
            scaled
            - jnp.mean(scaled, axis=-1, keepdims=True)
            - x_hat * jnp.mean(scaled * x_hat, axis=-1, keepdims=True)
        )
        grad_ref[rank] = (cot_ref[b].astype(F32) + d_input).astype(BF16)

    by_encoder(routed, where_ref, kind_ref, weight_copies(routed, where_ref, weights, wq, wo, sems), body)


def left_kernel(where_ref, kind_ref, ht_a, ht_b, left):
    g, c = where_ref[0], where_ref[2]
    count = ht_a.shape[0]
    rows = left.shape[2] // 8
    for far in range(2):
        kind = (g // 2) ^ far
        for i in range(2 * count):
            source = ht_a if i < count else ht_b
            keep = kind_ref[i] == kind
            for side in range(2):
                for z in range(4):
                    row = pl.multiple_of(((2 * z + c) * 2 + ((g % 2) ^ side)) * rows, 16)
                    value = source[i % count, pl.ds(row, rows), :]
                    at = (side * 4 + z) * rows
                    left[far, i // count, at : at + rows, (i % count) * LANES : (i % count + 1) * LANES] = (
                        jnp.where(keep, value, jnp.zeros_like(value))
                    )


def out_terms_kernel(where_ref, kind_ref, attnt_a, attnt_b, cot_a, cot_b, own_ref, sent_ref, left):
    g, z, c = where_ref[0], where_ref[1], where_ref[2]
    count = attnt_a.shape[0]
    rows = left.shape[2] // 4
    half_width = cot_a.shape[2] // 2
    for far in range(2):
        kind = (g // 2) ^ far
        for i in range(2 * count):
            source = attnt_a if i < count else attnt_b
            keep = kind_ref[i] == kind
            for step in range(4):
                row = pl.multiple_of((2 * lax.rem(z + step, 4) + c) * rows, 16)
                value = source[i % count, pl.ds(row, rows), :]
                left[far, i // count, step * rows : (step + 1) * rows, (i % count) * LANES : (i % count + 1) * LANES] = (
                    jnp.where(keep, value, jnp.zeros_like(value))
                )
    for far in range(2):
        for side in range(2):
            span = pl.ds(pl.multiple_of(((g % 2) ^ side) * half_width, LANES), half_width)
            total = dot_nn(left[far, 0], cot_a[:, :, span].reshape(-1, half_width))
            total += dot_nn(left[far, 1], cot_b[:, :, span].reshape(-1, half_width))
            total = total.reshape(4, rows, half_width)
            own_ref[2 * far + side] = total[0]
            for step in range(4):
                sent_ref[lax.rem(z + step, 4), 2 * far + side] = total[step].astype(BF16)


def qkv_terms_kernel(left, *rest):
    pairs, (y_ref, x_ref, own_ref, xa_ref, yb_ref) = rest[:6], rest[6:]
    rows = left.shape[2] // 8
    width, cut = pairs[0].shape[2], xa_ref.shape[2]
    chunk = 3 * LANES
    for far in range(2):
        for part in range(3):
            d_a, d_b = pairs[2 * part : 2 * part + 2]
            for low in range(0, width, chunk):
                size = min(chunk, width - low)
                span = slice(low, low + size)
                total = dot_nn(left[far, 0], d_a[:, :, span].reshape(-1, size))
                total += dot_nn(left[far, 1], d_b[:, :, span].reshape(-1, size))
                total = total.reshape(2, 4, rows, size)
                at = part * width + low
                first = slice(at, at + size)
                last = slice(at - cut, at - cut + size)
                if far == 0:
                    own_ref[:, :, first] = total[0]
                for side in range(2):
                    if (far, side) == (0, 0):
                        continue
                    if at < cut and far:
                        y_ref[side, :, :, first] = total[side].astype(BF16)
                    elif at < cut:
                        xa_ref[:, :, first] = total[side]
                    elif side:
                        x_ref[far, :, :, last] = total[side].astype(BF16)
                    else:
                        yb_ref[:, :, last] = total[side]


QKV_CUT = 1024
STEPS = ((slice(0, 512), slice(0, 512)), (slice(512, None), slice(512, None)))
OUT_CUT = 384


def left_factor(where, kinds, ht, ht_other):
    count, width, window = ht.shape
    return pl.pallas_call(
        left_kernel,
        out_shape=jax.ShapeDtypeStruct((2, 2, width // 2, count * window), BF16),
        in_specs=[SMEM, SMEM] + [VMEM] * 2,
        out_specs=VMEM,
        compiler_params=params(),
        cost_estimate=cost(0.01),
        name="left_factor",
    )(where, kinds, ht, ht_other)


def out_terms(where, kinds, *pairs):
    count, inner, window = pairs[0].shape
    rows, width = inner // 8, pairs[2].shape[2] // 2
    return pl.pallas_call(
        out_terms_kernel,
        out_shape=[
            jax.ShapeDtypeStruct((4, rows, width), F32),
            jax.ShapeDtypeStruct((4, 4, rows, width), BF16),
        ],
        in_specs=[SMEM, SMEM] + [VMEM] * len(pairs),
        out_specs=[VMEM] * 2,
        scratch_shapes=[pltpu.VMEM((2, 2, inner // 2, count * window), BF16)],
        compiler_params=params(),
        cost_estimate=cost(0.01),
        name="out_terms",
    )(where, kinds, *pairs)


def qkv_terms(left, *pairs):
    rows, columns = left.shape[2] // 8, 3 * pairs[0].shape[2]
    rest = columns - QKV_CUT
    return pl.pallas_call(
        qkv_terms_kernel,
        out_shape=[
            jax.ShapeDtypeStruct((2, 4, rows, QKV_CUT), BF16),
            jax.ShapeDtypeStruct((2, 4, rows, rest), BF16),
            jax.ShapeDtypeStruct((4, rows, columns), F32),
            jax.ShapeDtypeStruct((4, rows, QKV_CUT), F32),
            jax.ShapeDtypeStruct((4, rows, rest), F32),
        ],
        in_specs=[VMEM] * (1 + len(pairs)),
        out_specs=[VMEM] * 5,
        compiler_params=params(),
        cost_estimate=cost(0.01),
        name="qkv_terms",
    )(left, *pairs)


def flat(groups, shards, move):
    pairs = []
    for g in range(groups):
        for d in range(shards):
            to_g, to_d = move(g, d)
            pairs.append((g * shards + d, to_g * shards + to_d))
    return pairs


def routes(groups, shards):
    chips = shards // 2
    make = functools.partial(flat, groups, shards)
    return {
        "sibling": make(lambda g, d: (g, d ^ 1)),
        "x": make(lambda g, d: (g ^ 1, d)),
        "y": make(lambda g, d: (g ^ 2, d)),
        "z": [
            make(lambda g, d, s=s: (g, (d // 2 + s) % chips * 2 + d % 2)) for s in range(chips)
        ],
    }


def send(value, route):
    return lax.ppermute(value, AXES, route)


def tied(value, *others):
    return lax.optimization_barrier((value, *others))[0]


def gather_small(norm_gain, modality, route, z, c):
    kinds, rows = norm_gain.shape
    gains = norm_gain.astype(F32).reshape(1, -1)
    sibling = send(jnp.concatenate([gains, modality.astype(F32)[None]], axis=1), route["sibling"])
    others, kinds_other = sibling[:, : kinds * rows], sibling[0, kinds * rows :].astype(jnp.int32)
    pair = jnp.concatenate([jnp.where(c == 0, gains, others), jnp.where(c == 0, others, gains)], axis=0)
    chips = jnp.arange(4)[:, None, None]
    total = jnp.where(chips == z, pair[None], 0)
    for step in range(1, 4):
        total += jnp.where(chips == (z + 4 - step) % 4, send(pair, route["z"][step])[None], 0)
    return total.reshape(8, kinds, rows).transpose(1, 0, 2).reshape(kinds, -1), kinds_other


def quarter_of(qkv_weight, out_weight, q):
    rows, narrow = qkv_weight.shape[1] // 2, out_weight.shape[2] // 2
    own_qkv = lax.dynamic_slice(qkv_weight, (q // 2, q % 2 * rows, 0), (1, rows, qkv_weight.shape[2]))
    own_out = lax.dynamic_slice(out_weight, (q // 2, 0, q % 2 * narrow), (1, out_weight.shape[1], narrow))
    return jnp.concatenate([own_qkv, own_out], axis=2)


def quarters_of(qkv_weight, out_weight):
    kinds, rows, columns = qkv_weight.shape
    narrow = out_weight.shape[2] // 2
    return jnp.concatenate(
        [
            qkv_weight.reshape(4, rows // 2, columns),
            out_weight.reshape(kinds, -1, 2, narrow).transpose(0, 2, 1, 3).reshape(4, -1, narrow),
        ],
        axis=2,
    )


def send_terms(terms, route):
    to_y, to_x = terms[:2]
    return send(to_y, route["y"]), send(to_x, route["x"])


def reduce_plane(terms, arrived, route):
    _, _, own, x_term, y_term = terms
    from_y, from_x = arrived
    next_x = send((x_term + from_y[1].astype(F32)).astype(BF16), route["x"])
    next_y = send((y_term + from_x[1].astype(F32)).astype(BF16), route["y"])
    return own + jnp.concatenate(
        [
            from_y[0].astype(F32) + next_x.astype(F32),
            from_x[0].astype(F32) + next_y.astype(F32),
        ],
        axis=-1,
    )


def send_line(value):
    count = lax.axis_size("dp")
    lines = [list(range(core, count, 2)) for core in range(2)]
    return lax.all_to_all(value, "dp", split_axis=0, concat_axis=0, axis_index_groups=lines, tiled=True)


def add_line(own, arrived, z):
    others = jnp.arange(arrived.shape[0]).reshape((-1,) + (1,) * own.ndim) != z
    return own + jnp.sum(jnp.where(others, arrived.astype(F32), 0), axis=0)


def line_parts(total, z):
    parts = [lax.dynamic_index_in_dim(total, (z + step) % 4, 0, keepdims=False) for step in range(4)]
    return [parts[0]] + [part.astype(BF16) for part in parts[1:]]


def reduce_line(parts, route):
    return parts[0] + sum(send(parts[step], route["z"][step]).astype(F32) for step in range(1, 4))


def plane_terms(total, cut):
    first, second = total[..., :cut], total[..., cut:]
    return [
        first[2:].astype(BF16),
        jnp.stack([second[1], second[3]]).astype(BF16),
        total[0],
        first[1],
        second[2],
    ]


def both_halves(share, g, route):
    other = send(share.astype(BF16), route["x"]).astype(F32)
    return [jnp.where(g % 2 == i, share, other) for i in range(2)]


def whole_weights(qkv_weight, out_weight):
    return [
        lax.all_gather(qkv_weight, "dp", axis=1, tiled=True),
        lax.all_gather(out_weight, "dp", axis=1, tiled=True),
    ]


def summed_terms(kinds, h, dqkv, attn, cot):
    shards = lax.axis_size("dp")
    results = []
    for left, right in ((h, dqkv), (attn, cot)):
        parts = []
        for kind in range(2):
            keep = (kinds == kind)[:, None, None]
            parts.append(
                jnp.einsum("bwi,bwj->ij", jnp.where(keep, left, 0), right, preferred_element_type=F32)
            )
        total = lax.psum_scatter(
            jnp.stack(parts).reshape(2, shards, -1, right.shape[2]), "dp", scatter_dimension=1
        )
        total = lax.psum(total, "grp")
        results.append(lax.dynamic_index_in_dim(total, lax.axis_index("grp") // 2, 0, keepdims=False))
    return results


def shards(blocks, cotangent, modality, time_rank, qkv_weight, out_weight, norm_gain):
    groups, shard_count = lax.axis_size("grp"), lax.axis_size("dp")
    g, d = lax.axis_index("grp"), lax.axis_index("dp")
    z, c = d // 2, d % 2
    count, window, width = blocks.shape
    columns = qkv_weight.shape[2]
    inner = columns // 3
    routed = groups == 4 and shard_count == 8 and out_weight.shape[1] % 16 == 0
    where = jnp.stack([g, z, c]).astype(jnp.int32)
    rows = count * window

    def normed(blocks, gain):
        return pl.pallas_call(
            norm_kernel,
            out_shape=[
                jax.ShapeDtypeStruct(blocks.shape, BF16),
                jax.ShapeDtypeStruct((count, width, window), BF16),
            ],
            in_specs=[SMEM, VMEM, VMEM],
            out_specs=[VMEM] * 2,
            compiler_params=params(),
            cost_estimate=cost(0.01),
            name="norm",
        )(modality, blocks, gain)

    if routed:
        route = routes(groups, shard_count)

        def in_plane(held):
            return send(held, route["x"]), send(held, route["y"])

        def sibling(value, *after):
            return send(tied(value, *after) if after else value, route["sibling"])

        own = quarter_of(qkv_weight, out_weight, g)
        near = send(own, route["z"][1])
        gain, kinds_other = gather_small(tied(norm_gain, own), modality, route, z, c)
        near = tied(near, gain)
        far = send(near, route["z"][1])
        near_x, near_y = in_plane(near)
        h, ht = normed(tied(blocks, near), gain)
        quarters = quarters_of(tied(qkv_weight, near), out_weight)
        diagonal = lax.dynamic_slice_in_dim(quarters, g ^ 3, 1, 0)
        quarters_other = sibling(quarters)
        cot_other = sibling(cotangent, near)
        far = tied(far, near_x, near_y, h, quarters_other)
        far_x, far_y = in_plane(far)
        back = send(tied(own, far), route["z"][3])
        kinds = jnp.concatenate([modality, kinds_other])
        ht_other = sibling(ht, far)
        left = left_factor(where, kinds, ht, ht_other)
        near_other = sibling(near, far)
        near_x_other = sibling(near_x, near_other)
        near_y_other = sibling(near_y, near_other)
        back = tied(back, far_x, far_y, left, near_other)
        back_x, back_y = in_plane(back)
        near_across = send(tied(diagonal, back), route["z"][1])
        far_other = sibling(far, back)
        far_x_other = sibling(far_x, far_other)
        far_y_other = sibling(far_y, far_other)
        back_other = sibling(back, far_other)
        far_across = send(tied(far_x, back), route["y"])
        back_across = send(tied(diagonal, back), route["z"][3])
        weights = [quarters, quarters_other, near, near_other, near_x, near_x_other, near_y, near_y_other]
        weights += [near_across, sibling(near_across), far, far_other, far_x, far_x_other, far_y, far_y_other]
        weights += [far_across, sibling(far_across), back, back_other, back_x, sibling(back_x)]
        weights += [back_y, sibling(back_y), back_across, sibling(back_across)]
    else:
        gain = lax.all_gather(norm_gain, "dp", axis=1, tiled=True).astype(F32)
        weights = whole_weights(qkv_weight, out_weight)
        h, ht = normed(blocks, gain)
    n_weights = len(weights)
    weight_scratch = [
        pltpu.VMEM((2, width, columns), BF16),
        pltpu.VMEM((2, inner, width), BF16),
    ]
    weight_sems = pltpu.SemaphoreType.DMA((2, 32))

    attnt, dq, dk, dv = pl.pallas_call(
        functools.partial(layer_kernel, routed, n_weights),
        out_shape=[jax.ShapeDtypeStruct((count, inner, window), BF16)]
        + [jax.ShapeDtypeStruct((count, window, inner), BF16)] * 3,
        in_specs=[SMEM, SMEM, VMEM, VMEM] + [HBM] * n_weights,
        out_specs=[VMEM] * 4,
        scratch_shapes=weight_scratch
        + [pltpu.VMEM((window, columns), BF16), pltpu.VMEM((window, inner), BF16), weight_sems],
        compiler_params=params(),
        cost_estimate=cost(0.01),
        name="layer",
    )(where, modality, h, cotangent, *weights)

    def results(attnt):
        return pl.pallas_call(
            functools.partial(result_kernel, routed, n_weights),
            out_shape=[jax.ShapeDtypeStruct(blocks.shape, BF16)] * 2,
            in_specs=[SMEM] * 3 + [VMEM] * 7 + [HBM] * n_weights,
            out_specs=[VMEM] * 2,
            scratch_shapes=weight_scratch + [pltpu.VMEM((window, width), F32), weight_sems],
            compiler_params=params(),
            cost_estimate=cost(0.01),
            name="result",
        )(where, modality, time_rank, blocks, cotangent, gain, attnt, dq, dk, dv, *weights)

    if routed:
        dq_other, dk_other, dv_other, attnt_other = [
            send(part, route["sibling"]) for part in (dq, dk, dv, attnt)
        ]
        terms = qkv_terms(left, dq, dq_other, dk, dk_other, dv, dv_other)
        arrived = send_terms(terms, route)
        out_own, out_sent = out_terms(
            where, kinds, tied(attnt, terms[0]), attnt_other, cotangent, cot_other
        )
        out_arrived = send_line(out_sent)
        encoded, block_grad = results(tied(attnt, out_own))
        arrived = lax.optimization_barrier((*arrived, encoded))[:2]
        parts = []
        for first, last in STEPS:
            step_arrived = (arrived[0][..., first], arrived[1][..., last])
            own = jnp.concatenate([terms[2][..., :QKV_CUT][..., first], terms[2][..., QKV_CUT:][..., last]], axis=2)
            step_terms = (None, None, own, terms[3][..., first], terms[4][..., last])
            parts.append(line_parts(reduce_plane(step_terms, step_arrived, route), z))
        out_arrived = tied(out_arrived, *parts[0])
        terms = plane_terms(add_line(out_own, out_arrived, z), OUT_CUT)
        arrived = send_terms(terms, route)
        parts[1][0] = tied(parts[1][0], *arrived)
        shares = [reduce_line(part, route) for part in parts]
        shares[1] = jnp.concatenate([shares[1], reduce_plane(terms, arrived, route)], axis=1)
        first_halves, last_halves = [both_halves(share, g, route) for share in shares]
        cut = last_halves[0].shape[1] - cotangent.shape[2] // 2
        share_out = jnp.concatenate([half[:, cut:] for half in last_halves], axis=1)
        columns_of = [
            [half[:, :512] for half in first_halves],
            [half[:, :512] for half in last_halves],
            [half[:, 512:] for half in first_halves],
            [half[:, 512:cut] for half in last_halves],
        ]
        share_qkv = jnp.concatenate([jnp.concatenate(halves, axis=0) for halves in columns_of], axis=1)
    else:
        encoded, block_grad = results(attnt)
        share_qkv, share_out = summed_terms(
            modality, h, jnp.concatenate([dq, dk, dv], axis=2), attnt.transpose(0, 2, 1), cotangent
        )

    kind = g // 2
    own_weight = lax.dynamic_index_in_dim(qkv_weight, kind, 0, keepdims=False).astype(F32)
    own_gain = lax.dynamic_index_in_dim(norm_gain, kind, 0, keepdims=False).astype(F32)
    share_gain = jnp.sum(share_qkv * own_weight, axis=1) / own_gain

    return (encoded, block_grad, share_qkv[None], share_out[None], share_gain[None])


def solution(mesh):
    return jax.shard_map(
        shards,
        mesh=mesh,
        in_specs=(
            P(("grp", "dp"), None, None),
            P(("grp", "dp"), None, None),
            P(("grp", "dp")),
            P(("grp", "dp")),
            P(None, "dp", None),
            P(None, "dp", None),
            P(None, "dp"),
        ),
        out_specs=(
            P(("grp", "dp"), None, None),
            P(("grp", "dp"), None, None),
            P("grp", "dp", None),
            P("grp", "dp", None),
            P("grp", "dp"),
        ),
        check_vma=False,
    )
```

```python
import functools
import math

import jax
import jax.numpy as jnp
from jax import lax
from jax.experimental import pallas as pl
from jax.experimental.pallas import tpu as pltpu
from jax.sharding import PartitionSpec as P

A_HEADS = 10
A_SIZE = 64
V_HEADS = 8
V_SIZE = 80
VWIN = 64
EPSILON = 1e-05
LANES = 128
AXES = ("grp", "dp")
VMEM_LIMIT = 60 * 1024 * 1024
BF16 = jnp.bfloat16
F32 = jnp.float32

VMEM = pl.BlockSpec(memory_space=pltpu.VMEM)
SMEM = pl.BlockSpec(memory_space=pltpu.SMEM)
HBM = pl.BlockSpec(memory_space=pl.ANY)


def params():
    return pltpu.CompilerParams(vmem_limit_bytes=VMEM_LIMIT)


def cost(microseconds):
    return pl.CostEstimate(flops=int(microseconds * 1.15e9), bytes_accessed=0, transcendentals=0)


def dot_nn(a, b):
    return lax.dot_general(a, b, (((1,), (0,)), ((), ())), preferred_element_type=F32)


def dot_nt(a, b):
    return lax.dot_general(a, b, (((1,), (1,)), ((), ())), preferred_element_type=F32)


def dot_tn(a, b):
    return lax.dot_general(a, b, (((0,), (0,)), ((), ())), preferred_element_type=F32)


def normalise(x):
    mean = jnp.mean(x, axis=-1, keepdims=True)
    centered = x - mean
    inverse = lax.rsqrt(jnp.mean(centered * centered, axis=-1, keepdims=True) + EPSILON)
    return centered * inverse, inverse


def norm_kernel(kind_ref, x_ref, gain_ref, h_ref, ht_ref):
    def body(b, carry):
        x_hat, _ = normalise(x_ref[b].astype(F32))
        h = (x_hat * gain_ref[pl.ds(kind_ref[b], 1), :]).astype(BF16)
        h_ref[b] = h
        ht_ref[b] = h.T
        return carry

    lax.fori_loop(0, x_ref.shape[0], body, 0)


def attend(b, heads, size, window, qkv, da, attnt_ref, dq_ref, dk_ref, dv_ref):
    rows = qkv.shape[0]
    inner = heads * size
    scale = 1.0 / math.sqrt(size)
    same = None
    if window < rows:
        key = lax.broadcasted_iota(jnp.int32, (rows, 2 * rows), 0) // window
        query = lax.broadcasted_iota(jnp.int32, (rows, 2 * rows), 1) % rows // window
        same = key == query
    sums = {}

    def add(name, tile, value):
        known = sums.get((name, tile))
        sums[name, tile] = value if known is None else known + value

    for head in range(0, heads, 2):
        first, last = head * size // LANES, ((head + 2) * size - 1) // LANES + 1
        low, wide = first * LANES, (last - first) * LANES
        lane = lax.broadcasted_iota(jnp.int32, (rows, wide), 1) + low
        row = lax.broadcasted_iota(jnp.int32, (wide, rows), 0) + low
        lanes = [(lane >= h * size) & (lane < (h + 1) * size) for h in (head, head + 1)]
        bands = [(row >= h * size) & (row < (h + 1) * size) for h in (head, head + 1)]
        q, k, v = (qkv[:, at + low : at + low + wide] for at in (0, inner, 2 * inner))
        g = da[:, low : low + wide]
        q_pair = jnp.concatenate([jnp.where(mask, q, 0) for mask in lanes], axis=0)
        g_pair = jnp.concatenate([jnp.where(mask, g, 0) for mask in lanes], axis=0)
        scores = dot_nt(k, q_pair) * scale
        if same is not None:
            scores = jnp.where(same, scores, -1e30)
        exponent = jnp.exp(scores - jnp.max(scores, axis=0, keepdims=True))
        probs = exponent * (1.0 / jnp.sum(exponent, axis=0, keepdims=True))
        d_probs = dot_nt(v, g_pair)
        mean = jnp.sum(d_probs * probs, axis=0, keepdims=True)
        d_scores = (probs * (d_probs - mean) * scale).astype(BF16)
        probs = probs.astype(BF16)
        d_v = dot_nn(probs, g_pair)
        d_k = dot_nn(d_scores, q_pair)
        vt, kt = v.T, k.T
        mixed = dot_nn(
            jnp.concatenate([jnp.where(band, vt, 0) for band in bands], axis=1),
            jnp.concatenate([probs[:, :rows], probs[:, rows:]], axis=0),
        )
        d_q = dot_nn(
            jnp.concatenate([jnp.where(band, kt, 0) for band in bands], axis=1),
            jnp.concatenate([d_scores[:, :rows], d_scores[:, rows:]], axis=0),
        )
        for tile in range(first, last):
            span = slice(tile * LANES - low, (tile + 1) * LANES - low)
            add("v", tile, d_v[:, span])
            add("k", tile, d_k[:, span])
            add("q", tile, d_q[span])
            add("o", tile, mixed[span])
        for tile in range(first, last):
            span = slice(tile * LANES, (tile + 1) * LANES)
            if (head + 2) * size >= (tile + 1) * LANES:
                dv_ref[b, :, span] = sums.pop(("v", tile)).astype(BF16)
                dk_ref[b, :, span] = sums.pop(("k", tile)).astype(BF16)
                dq_ref[b, :, span] = sums.pop(("q", tile)).astype(BF16).T
                attnt_ref[b, span, :] = sums.pop(("o", tile)).astype(BF16)


def routed_copies(where_ref, refs, wq, wo, sems):
    g, z, c = where_ref[0], where_ref[1], where_ref[2]
    half_rows, wide, narrow = refs[0].shape[1], wq.shape[2], wo.shape[2] // 2
    groups = [(2 + 8 * i + 2 * other, other, step) for i, step in enumerate((3, 2, 1)) for other in range(4)]
    by_kind = []
    for far in range(2):
        kind = (g // 2) ^ far
        first, second = [], []
        for side in range(2):
            half = (g % 2) ^ side
            found = [(refs[i], 2 * kind + half, 2 * z + core) for i, core in ((0, c), (1, 1 - c))]
            for i, other, step in groups:
                if other == 2 * far + side:
                    chip = 2 * lax.rem(z + step, 4)
                    found += [(refs[i], 0, chip + c), (refs[i + 1], 0, chip + 1 - c)]
            for ref, at, shard in found:
                row = pl.multiple_of((shard * 2 + half) * half_rows, 16)
                out_row = pl.multiple_of(shard * half_rows, 16)
                column = pl.multiple_of(half * narrow, LANES)
                first.append(
                    pltpu.make_async_copy(
                        ref.at[at, :, pl.ds(0, wide)],
                        wq.at[kind, pl.ds(row, half_rows), :],
                        sems.at[far, len(first)],
                    )
                )
                second.append(
                    pltpu.make_async_copy(
                        ref.at[at, :, pl.ds(wide, narrow)],
                        wo.at[kind, pl.ds(out_row, half_rows), pl.ds(column, narrow)],
                        sems.at[far, 16 + len(second)],
                    )
                )
        by_kind.append(first + second)
    return by_kind


def weight_copies(routed, where_ref, refs, wq, wo, sems):
    if routed:
        return routed_copies(where_ref, refs, wq, wo, sems)
    return [
        [
            pltpu.make_async_copy(ref.at[kind], to.at[kind], sems.at[kind, i])
            for i, (ref, to) in enumerate(zip(refs, (wq, wo)))
        ]
        for kind in range(2)
    ]


def by_encoder(routed, where_ref, kind_ref, copies, body):
    for group in copies:
        for copy in group:
            copy.start()
    blocks = kind_ref.shape[0]
    first = where_ref[0] // 2 if routed else 0

    def step(i, carry):
        b, far = lax.rem(i, blocks), lax.div(i, blocks)
        for turn, group in enumerate(copies):

            @pl.when(i == turn * blocks)
            def _():
                for copy in group:
                    copy.wait()

        kind = first ^ far

        @pl.when(kind_ref[b] == kind)
        def _():
            body(b, kind)

        return carry

    lax.fori_loop(0, 2 * blocks, step, 0)


def layer_kernel(routed, n_weights, where_ref, kind_ref, h_ref, cot_ref, *rest):
    weights, rest = rest[:n_weights], rest[n_weights:]
    attnt_ref, dq_ref, dk_ref, dv_ref, wq, wo, qkv_ref, da_ref, sems = rest
    chunk = 3 * LANES

    def body(b, kind):
        for at in range(0, wq.shape[2], chunk):
            qkv_ref[:, at : at + chunk] = dot_nn(h_ref[b], wq[kind, :, at : at + chunk]).astype(BF16)
        for at in range(0, wo.shape[1], LANES):
            da_ref[:, at : at + LANES] = dot_nt(cot_ref[b], wo[kind, at : at + LANES, :]).astype(BF16)

        @pl.when(kind == 0)
        def _():
            attend(b, A_HEADS, A_SIZE, qkv_ref.shape[0], qkv_ref, da_ref, attnt_ref, dq_ref, dk_ref, dv_ref)

        @pl.when(kind != 0)
        def _():
            attend(b, V_HEADS, V_SIZE, VWIN, qkv_ref, da_ref, attnt_ref, dq_ref, dk_ref, dv_ref)

    by_encoder(routed, where_ref, kind_ref, weight_copies(routed, where_ref, weights, wq, wo, sems), body)


def result_kernel(routed, n_weights, where_ref, kind_ref, rank_ref, x_ref, cot_ref, gain_ref, attnt_ref, dq_ref, dk_ref, dv_ref, *rest):
    weights, rest = rest[:n_weights], rest[n_weights:]
    encoded_ref, grad_ref, wq, wo, wide_ref, sems = rest
    inner = dq_ref.shape[2]
    chunk = 2 * LANES
    width = x_ref.shape[2]

    def body(b, kind):
        rank = rank_ref[b]
        attn = attnt_ref[b].T
        for at in range(0, width, chunk):
            span = slice(at, at + chunk)
            encoded_ref[rank, :, span] = (
                x_ref[b, :, span].astype(F32) + dot_nn(attn, wo[kind, :, span])
            ).astype(BF16)
            wide_ref[:, span] = (
                dot_nt(dq_ref[b], wq[kind, span, :inner])
                + dot_nt(dk_ref[b], wq[kind, span, inner : 2 * inner])
                + dot_nt(dv_ref[b], wq[kind, span, 2 * inner :])
            )
        x_hat, inverse = normalise(x_ref[b].astype(F32))
        scaled = wide_ref[...] * gain_ref[pl.ds(kind, 1), :]
        d_input = inverse * (
            scaled
            - jnp.mean(scaled, axis=-1, keepdims=True)
            - x_hat * jnp.mean(scaled * x_hat, axis=-1, keepdims=True)
        )
        grad_ref[rank] = (cot_ref[b].astype(F32) + d_input).astype(BF16)

    by_encoder(routed, where_ref, kind_ref, weight_copies(routed, where_ref, weights, wq, wo, sems), body)


def left_kernel(where_ref, kind_ref, ht_a, ht_b, left):
    g, c = where_ref[0], where_ref[2]
    count = ht_a.shape[0]
    rows = left.shape[2] // 8
    for far in range(2):
        kind = (g // 2) ^ far
        for i in range(2 * count):
            source = ht_a if i < count else ht_b
            keep = kind_ref[i] == kind
            for side in range(2):
                for z in range(4):
                    row = pl.multiple_of(((2 * z + c) * 2 + ((g % 2) ^ side)) * rows, 16)
                    value = source[i % count, pl.ds(row, rows), :]
                    at = (side * 4 + z) * rows
                    left[far, i // count, at : at + rows, (i % count) * LANES : (i % count + 1) * LANES] = (
                        jnp.where(keep, value, jnp.zeros_like(value))
                    )


def out_terms_kernel(where_ref, kind_ref, attnt_a, attnt_b, cot_a, cot_b, own_ref, far_ref, sent_ref, left):
    g, z, c = where_ref[0], where_ref[1], where_ref[2]
    count = attnt_a.shape[0]
    rows = left.shape[2] // 4
    half_width = cot_a.shape[2] // 2
    for far in range(2):
        kind = (g // 2) ^ far
        for i in range(2 * count):
            source = attnt_a if i < count else attnt_b
            keep = kind_ref[i] == kind
            for step in range(4):
                row = pl.multiple_of((2 * (z ^ step) + c) * rows, 16)
                value = source[i % count, pl.ds(row, rows), :]
                left[far, i // count, step * rows : (step + 1) * rows, (i % count) * LANES : (i % count + 1) * LANES] = (
                    jnp.where(keep, value, jnp.zeros_like(value))
                )
    for far in range(2):
        for side in range(2):
            span = pl.ds(pl.multiple_of(((g % 2) ^ side) * half_width, LANES), half_width)
            total = dot_nn(left[far, 0], cot_a[:, :, span].reshape(-1, half_width))
            total += dot_nn(left[far, 1], cot_b[:, :, span].reshape(-1, half_width))
            total = total.reshape(4, rows, half_width)
            own_ref[2 * far + side] = total[0]
            far_ref[2 * far + side] = total[2]
            sent_ref[0, 2 * far + side] = total[1].astype(BF16)
            sent_ref[1, 2 * far + side] = total[3].astype(BF16)


def qkv_terms_kernel(left, *rest):
    pairs, (y_ref, x_ref, own_ref, xa_ref, yb_ref) = rest[:6], rest[6:]
    rows = left.shape[2] // 8
    width, cut = pairs[0].shape[2], xa_ref.shape[2]
    chunk = 3 * LANES
    for far in range(2):
        for part in range(3):
            d_a, d_b = pairs[2 * part : 2 * part + 2]
            for low in range(0, width, chunk):
                size = min(chunk, width - low)
                span = slice(low, low + size)
                total = dot_nn(left[far, 0], d_a[:, :, span].reshape(-1, size))
                total += dot_nn(left[far, 1], d_b[:, :, span].reshape(-1, size))
                total = total.reshape(2, 4, rows, size)
                at = part * width + low
                first = slice(at, at + size)
                last = slice(at - cut, at - cut + size)
                if far == 0:
                    own_ref[:, :, first] = total[0]
                for side in range(2):
                    if (far, side) == (0, 0):
                        continue
                    if at < cut and far:
                        y_ref[side, :, :, first] = total[side].astype(BF16)
                    elif at < cut:
                        xa_ref[:, :, first] = total[side]
                    elif side:
                        x_ref[far, :, :, last] = total[side].astype(BF16)
                    else:
                        yb_ref[:, :, last] = total[side]


QKV_CUT = 1024
STEPS = ((slice(0, 512), slice(0, 512)), (slice(512, None), slice(512, None)))
OUT_CUT = 384


def left_factor(where, kinds, ht, ht_other):
    count, width, window = ht.shape
    return pl.pallas_call(
        left_kernel,
        out_shape=jax.ShapeDtypeStruct((2, 2, width // 2, count * window), BF16),
        in_specs=[SMEM, SMEM] + [VMEM] * 2,
        out_specs=VMEM,
        compiler_params=params(),
        cost_estimate=cost(0.01),
        name="left_factor",
    )(where, kinds, ht, ht_other)


def out_terms(where, kinds, *pairs):
    count, inner, window = pairs[0].shape
    rows, width = inner // 8, pairs[2].shape[2] // 2
    return pl.pallas_call(
        out_terms_kernel,
        out_shape=[
            jax.ShapeDtypeStruct((4, rows, width), F32),
            jax.ShapeDtypeStruct((4, rows, width), F32),
            jax.ShapeDtypeStruct((2, 4, rows, width), BF16),
        ],
        in_specs=[SMEM, SMEM] + [VMEM] * len(pairs),
        out_specs=[VMEM] * 3,
        scratch_shapes=[pltpu.VMEM((2, 2, inner // 2, count * window), BF16)],
        compiler_params=params(),
        cost_estimate=cost(0.01),
        name="out_terms",
    )(where, kinds, *pairs)


def qkv_terms(left, *pairs):
    rows, columns = left.shape[2] // 8, 3 * pairs[0].shape[2]
    rest = columns - QKV_CUT
    return pl.pallas_call(
        qkv_terms_kernel,
        out_shape=[
            jax.ShapeDtypeStruct((2, 4, rows, QKV_CUT), BF16),
            jax.ShapeDtypeStruct((2, 4, rows, rest), BF16),
            jax.ShapeDtypeStruct((4, rows, columns), F32),
            jax.ShapeDtypeStruct((4, rows, QKV_CUT), F32),
            jax.ShapeDtypeStruct((4, rows, rest), F32),
        ],
        in_specs=[VMEM] * (1 + len(pairs)),
        out_specs=[VMEM] * 5,
        compiler_params=params(),
        cost_estimate=cost(0.01),
        name="qkv_terms",
    )(left, *pairs)


def flat(groups, shards, move):
    pairs = []
    for g in range(groups):
        for d in range(shards):
            to_g, to_d = move(g, d)
            pairs.append((g * shards + d, to_g * shards + to_d))
    return pairs


def routes(groups, shards):
    chips = shards // 2
    make = functools.partial(flat, groups, shards)
    return {
        "sibling": make(lambda g, d: (g, d ^ 1)),
        "x": make(lambda g, d: (g ^ 1, d)),
        "y": make(lambda g, d: (g ^ 2, d)),
        "z1": make(lambda g, d: (g, d ^ 2)),
        "z2": make(lambda g, d: (g, d ^ 4)),
        "z": [
            make(lambda g, d, s=s: (g, (d // 2 + s) % chips * 2 + d % 2)) for s in range(chips)
        ],
    }


def send(value, route):
    return lax.ppermute(value, AXES, route)


def tied(value, *others):
    return lax.optimization_barrier((value, *others))[0]


def gather_small(norm_gain, modality, route, z, c):
    kinds, rows = norm_gain.shape
    gains = norm_gain.astype(F32).reshape(1, -1)
    sibling = send(jnp.concatenate([gains, modality.astype(F32)[None]], axis=1), route["sibling"])
    others, kinds_other = sibling[:, : kinds * rows], sibling[0, kinds * rows :].astype(jnp.int32)
    pair = jnp.concatenate([jnp.where(c == 0, gains, others), jnp.where(c == 0, others, gains)], axis=0)
    chips = jnp.arange(4)[:, None, None]
    total = jnp.where(chips == z, pair[None], 0)
    for step in range(1, 4):
        total += jnp.where(chips == (z + 4 - step) % 4, send(pair, route["z"][step])[None], 0)
    return total.reshape(8, kinds, rows).transpose(1, 0, 2).reshape(kinds, -1), kinds_other


def quarter_of(qkv_weight, out_weight, q):
    rows, narrow = qkv_weight.shape[1] // 2, out_weight.shape[2] // 2
    own_qkv = lax.dynamic_slice(qkv_weight, (q // 2, q % 2 * rows, 0), (1, rows, qkv_weight.shape[2]))
    own_out = lax.dynamic_slice(out_weight, (q // 2, 0, q % 2 * narrow), (1, out_weight.shape[1], narrow))
    return jnp.concatenate([own_qkv, own_out], axis=2)


def quarters_of(qkv_weight, out_weight):
    kinds, rows, columns = qkv_weight.shape
    narrow = out_weight.shape[2] // 2
    return jnp.concatenate(
        [
            qkv_weight.reshape(4, rows // 2, columns),
            out_weight.reshape(kinds, -1, 2, narrow).transpose(0, 2, 1, 3).reshape(4, -1, narrow),
        ],
        axis=2,
    )


def send_terms(terms, route):
    to_y, to_x = terms[:2]
    return send(to_y, route["y"]), send(to_x, route["x"])


def reduce_plane(terms, arrived, route):
    _, _, own, x_term, y_term = terms
    from_y, from_x = arrived
    next_x = send((x_term + from_y[1].astype(F32)).astype(BF16), route["x"])
    next_y = send((y_term + from_x[1].astype(F32)).astype(BF16), route["y"])
    return own + jnp.concatenate(
        [
            from_y[0].astype(F32) + next_x.astype(F32),
            from_x[0].astype(F32) + next_y.astype(F32),
        ],
        axis=-1,
    )


def line_parts(total, z):
    parts = [lax.dynamic_index_in_dim(total, (z + step) % 4, 0, keepdims=False) for step in range(4)]
    return [parts[0]] + [part.astype(BF16) for part in parts[1:]]


def send_line(parts, route):
    return [send(parts[step], route["z"][step]) for step in range(1, 4)]


def add_line(own, arrived):
    return own + sum(part.astype(F32) for part in arrived)


def plane_terms(total, cut):
    first, second = total[..., :cut], total[..., cut:]
    return [
        first[2:].astype(BF16),
        jnp.stack([second[1], second[3]]).astype(BF16),
        total[0],
        first[1],
        second[2],
    ]


def both_halves(share, g, route):
    other = send(share.astype(BF16), route["x"]).astype(F32)
    return [jnp.where(g % 2 == i, share, other) for i in range(2)]


def whole_weights(qkv_weight, out_weight):
    return [
        lax.all_gather(qkv_weight, "dp", axis=1, tiled=True),
        lax.all_gather(out_weight, "dp", axis=1, tiled=True),
    ]


def summed_terms(kinds, h, dqkv, attn, cot):
    shards = lax.axis_size("dp")
    results = []
    for left, right in ((h, dqkv), (attn, cot)):
        parts = []
        for kind in range(2):
            keep = (kinds == kind)[:, None, None]
            parts.append(
                jnp.einsum("bwi,bwj->ij", jnp.where(keep, left, 0), right, preferred_element_type=F32)
            )
        total = lax.psum_scatter(
            jnp.stack(parts).reshape(2, shards, -1, right.shape[2]), "dp", scatter_dimension=1
        )
        total = lax.psum(total, "grp")
        results.append(lax.dynamic_index_in_dim(total, lax.axis_index("grp") // 2, 0, keepdims=False))
    return results


def shards(blocks, cotangent, modality, time_rank, qkv_weight, out_weight, norm_gain):
    groups, shard_count = lax.axis_size("grp"), lax.axis_size("dp")
    g, d = lax.axis_index("grp"), lax.axis_index("dp")
    z, c = d // 2, d % 2
    count, window, width = blocks.shape
    columns = qkv_weight.shape[2]
    inner = columns // 3
    routed = groups == 4 and shard_count == 8 and out_weight.shape[1] % 16 == 0
    where = jnp.stack([g, z, c]).astype(jnp.int32)
    rows = count * window

    def normed(blocks, gain):
        return pl.pallas_call(
            norm_kernel,
            out_shape=[
                jax.ShapeDtypeStruct(blocks.shape, BF16),
                jax.ShapeDtypeStruct((count, width, window), BF16),
            ],
            in_specs=[SMEM, VMEM, VMEM],
            out_specs=[VMEM] * 2,
            compiler_params=params(),
            cost_estimate=cost(0.01),
            name="norm",
        )(modality, blocks, gain)

    if routed:
        route = routes(groups, shard_count)

        def in_plane(held):
            return send(held, route["x"]), send(held, route["y"])

        def sibling(value, *after):
            return send(tied(value, *after) if after else value, route["sibling"])

        own = quarter_of(qkv_weight, out_weight, g)
        near = send(own, route["z"][1])
        gain, kinds_other = gather_small(tied(norm_gain, own), modality, route, z, c)
        near = tied(near, gain)
        far = send(near, route["z"][1])
        near_x, near_y = in_plane(near)
        h, ht = normed(tied(blocks, near), gain)
        quarters = quarters_of(tied(qkv_weight, near), out_weight)
        diagonal = lax.dynamic_slice_in_dim(quarters, g ^ 3, 1, 0)
        quarters_other = sibling(quarters)
        cot_other = sibling(cotangent, near)
        far = tied(far, near_x, near_y, h, quarters_other)
        far_x, far_y = in_plane(far)
        back = send(tied(own, far), route["z"][3])
        kinds = jnp.concatenate([modality, kinds_other])
        ht_other = sibling(ht, far)
        left = left_factor(where, kinds, ht, ht_other)
        near_other = sibling(near, far)
        near_x_other = sibling(near_x, near_other)
        near_y_other = sibling(near_y, near_other)
        back = tied(back, far_x, far_y, left, near_other)
        back_x, back_y = in_plane(back)
        near_across = send(tied(diagonal, back), route["z"][1])
        far_other = sibling(far, back)
        far_x_other = sibling(far_x, far_other)
        far_y_other = sibling(far_y, far_other)
        back_other = sibling(back, far_other)
        far_across = send(tied(far_x, back), route["y"])
        back_across = send(tied(diagonal, back), route["z"][3])
        weights = [quarters, quarters_other, near, near_other, near_x, near_x_other, near_y, near_y_other]
        weights += [near_across, sibling(near_across), far, far_other, far_x, far_x_other, far_y, far_y_other]
        weights += [far_across, sibling(far_across), back, back_other, back_x, sibling(back_x)]
        weights += [back_y, sibling(back_y), back_across, sibling(back_across)]
    else:
        gain = lax.all_gather(norm_gain, "dp", axis=1, tiled=True).astype(F32)
        weights = whole_weights(qkv_weight, out_weight)
        h, ht = normed(blocks, gain)
    n_weights = len(weights)
    weight_scratch = [
        pltpu.VMEM((2, width, columns), BF16),
        pltpu.VMEM((2, inner, width), BF16),
    ]
    weight_sems = pltpu.SemaphoreType.DMA((2, 32))

    attnt, dq, dk, dv = pl.pallas_call(
        functools.partial(layer_kernel, routed, n_weights),
        out_shape=[jax.ShapeDtypeStruct((count, inner, window), BF16)]
        + [jax.ShapeDtypeStruct((count, window, inner), BF16)] * 3,
        in_specs=[SMEM, SMEM, VMEM, VMEM] + [HBM] * n_weights,
        out_specs=[VMEM] * 4,
        scratch_shapes=weight_scratch
        + [pltpu.VMEM((window, columns), BF16), pltpu.VMEM((window, inner), BF16), weight_sems],
        compiler_params=params(),
        cost_estimate=cost(0.01),
        name="layer",
    )(where, modality, h, cotangent, *weights)

    def results(attnt):
        return pl.pallas_call(
            functools.partial(result_kernel, routed, n_weights),
            out_shape=[jax.ShapeDtypeStruct(blocks.shape, BF16)] * 2,
            in_specs=[SMEM] * 3 + [VMEM] * 7 + [HBM] * n_weights,
            out_specs=[VMEM] * 2,
            scratch_shapes=weight_scratch + [pltpu.VMEM((window, width), F32), weight_sems],
            compiler_params=params(),
            cost_estimate=cost(0.01),
            name="result",
        )(where, modality, time_rank, blocks, cotangent, gain, attnt, dq, dk, dv, *weights)

    if routed:
        dq_other, dk_other, dv_other, attnt_other = [
            send(part, route["sibling"]) for part in (dq, dk, dv, attnt)
        ]
        terms = qkv_terms(left, dq, dq_other, dk, dk_other, dv, dv_other)
        arrived = send_terms(terms, route)
        out_own, out_far, out_sent = out_terms(
            where, kinds, tied(attnt, terms[0]), attnt_other, cotangent, cot_other
        )
        out_near = send(out_sent, route["z1"])
        encoded, block_grad = results(tied(attnt, out_own))
        out_near, *arrived = lax.optimization_barrier((out_near, *arrived, encoded))[:3]
        parts = []
        for first, last in STEPS:
            step_arrived = (arrived[0][..., first], arrived[1][..., last])
            own = jnp.concatenate([terms[2][..., :QKV_CUT][..., first], terms[2][..., QKV_CUT:][..., last]], axis=2)
            step_terms = (None, None, own, terms[3][..., first], terms[4][..., last])
            parts.append(line_parts(reduce_plane(step_terms, step_arrived, route), z))
        out_next = send((out_far + out_near[1].astype(F32)).astype(BF16), route["z2"])
        shares = [add_line(part[0], send_line(part, route)) for part in parts]
        out_total = tied(out_own + out_near[0].astype(F32) + out_next.astype(F32), *parts[1])
        terms = plane_terms(out_total, OUT_CUT)
        share = reduce_plane(terms, send_terms(terms, route), route)
        share_out = jnp.concatenate(both_halves(share, g, route), axis=1)
        (first_a, first_b), (last_a, last_b) = [
            tuple(zip(*[(half[:, :512], half[:, 512:]) for half in both_halves(share, g, route)]))
            for share in shares
        ]
        share_qkv = jnp.concatenate(
            [jnp.concatenate(halves, axis=0) for halves in (first_a, last_a, first_b, last_b)], axis=1
        )
    else:
        encoded, block_grad = results(attnt)
        share_qkv, share_out = summed_terms(
            modality, h, jnp.concatenate([dq, dk, dv], axis=2), attnt.transpose(0, 2, 1), cotangent
        )

    kind = g // 2
    own_weight = lax.dynamic_index_in_dim(qkv_weight, kind, 0, keepdims=False).astype(F32)
    own_gain = lax.dynamic_index_in_dim(norm_gain, kind, 0, keepdims=False).astype(F32)
    share_gain = jnp.sum(share_qkv * own_weight, axis=1) / own_gain

    return (encoded, block_grad, share_qkv[None], share_out[None], share_gain[None])


def solution(mesh):
    return jax.shard_map(
        shards,
        mesh=mesh,
        in_specs=(
            P(("grp", "dp"), None, None),
            P(("grp", "dp"), None, None),
            P(("grp", "dp")),
            P(("grp", "dp")),
            P(None, "dp", None),
            P(None, "dp", None),
            P(None, "dp"),
        ),
        out_specs=(
            P(("grp", "dp"), None, None),
            P(("grp", "dp"), None, None),
            P("grp", "dp", None),
            P("grp", "dp", None),
            P("grp", "dp"),
        ),
        check_vma=False,
    )
```

```python
import functools
import math

import jax
import jax.numpy as jnp
from jax import lax
from jax.experimental import pallas as pl
from jax.experimental.pallas import tpu as pltpu
from jax.sharding import PartitionSpec as P

A_HEADS = 10
A_SIZE = 64
V_HEADS = 8
V_SIZE = 80
VWIN = 64
EPSILON = 1e-05
LANES = 128
AXES = ("grp", "dp")
VMEM_LIMIT = 60 * 1024 * 1024
BF16 = jnp.bfloat16
F32 = jnp.float32

VMEM = pl.BlockSpec(memory_space=pltpu.VMEM)
SMEM = pl.BlockSpec(memory_space=pltpu.SMEM)
HBM = pl.BlockSpec(memory_space=pl.ANY)


def params():
    return pltpu.CompilerParams(vmem_limit_bytes=VMEM_LIMIT)


def cost(microseconds):
    return pl.CostEstimate(flops=int(microseconds * 1.15e9), bytes_accessed=0, transcendentals=0)


def dot_nn(a, b):
    return lax.dot_general(a, b, (((1,), (0,)), ((), ())), preferred_element_type=F32)


def dot_nt(a, b):
    return lax.dot_general(a, b, (((1,), (1,)), ((), ())), preferred_element_type=F32)


def dot_tn(a, b):
    return lax.dot_general(a, b, (((0,), (0,)), ((), ())), preferred_element_type=F32)


def normalise(x):
    mean = jnp.mean(x, axis=-1, keepdims=True)
    centered = x - mean
    inverse = lax.rsqrt(jnp.mean(centered * centered, axis=-1, keepdims=True) + EPSILON)
    return centered * inverse, inverse


def norm_kernel(kind_ref, x_ref, gain_ref, h_ref, ht_ref):
    def body(b, carry):
        x_hat, _ = normalise(x_ref[b].astype(F32))
        h = (x_hat * gain_ref[pl.ds(kind_ref[b], 1), :]).astype(BF16)
        h_ref[b] = h
        ht_ref[b] = h.T
        return carry

    lax.fori_loop(0, x_ref.shape[0], body, 0)


def attend(b, heads, size, window, qkv, da, attnt_ref, dq_ref, dk_ref, dv_ref):
    rows = qkv.shape[0]
    inner = heads * size
    scale = 1.0 / math.sqrt(size)
    same = None
    if window < rows:
        key = lax.broadcasted_iota(jnp.int32, (rows, 2 * rows), 0) // window
        query = lax.broadcasted_iota(jnp.int32, (rows, 2 * rows), 1) % rows // window
        same = key == query
    sums = {}

    def add(name, tile, value):
        known = sums.get((name, tile))
        sums[name, tile] = value if known is None else known + value

    for head in range(0, heads, 2):
        first, last = head * size // LANES, ((head + 2) * size - 1) // LANES + 1
        low, wide = first * LANES, (last - first) * LANES
        lane = lax.broadcasted_iota(jnp.int32, (rows, wide), 1) + low
        row = lax.broadcasted_iota(jnp.int32, (wide, rows), 0) + low
        lanes = [(lane >= h * size) & (lane < (h + 1) * size) for h in (head, head + 1)]
        bands = [(row >= h * size) & (row < (h + 1) * size) for h in (head, head + 1)]
        q, k, v = (qkv[:, at + low : at + low + wide] for at in (0, inner, 2 * inner))
        g = da[:, low : low + wide]
        q_pair = jnp.concatenate([jnp.where(mask, q, 0) for mask in lanes], axis=0)
        g_pair = jnp.concatenate([jnp.where(mask, g, 0) for mask in lanes], axis=0)
        scores = dot_nt(k, q_pair) * scale
        if same is not None:
            scores = jnp.where(same, scores, -1e30)
        exponent = jnp.exp(scores - jnp.max(scores, axis=0, keepdims=True))
        probs = exponent * (1.0 / jnp.sum(exponent, axis=0, keepdims=True))
        d_probs = dot_nt(v, g_pair)
        mean = jnp.sum(d_probs * probs, axis=0, keepdims=True)
        d_scores = (probs * (d_probs - mean) * scale).astype(BF16)
        probs = probs.astype(BF16)
        d_v = dot_nn(probs, g_pair)
        d_k = dot_nn(d_scores, q_pair)
        vt, kt = v.T, k.T
        mixed = dot_nn(
            jnp.concatenate([jnp.where(band, vt, 0) for band in bands], axis=1),
            jnp.concatenate([probs[:, :rows], probs[:, rows:]], axis=0),
        )
        d_q = dot_nn(
            jnp.concatenate([jnp.where(band, kt, 0) for band in bands], axis=1),
            jnp.concatenate([d_scores[:, :rows], d_scores[:, rows:]], axis=0),
        )
        for tile in range(first, last):
            span = slice(tile * LANES - low, (tile + 1) * LANES - low)
            add("v", tile, d_v[:, span])
            add("k", tile, d_k[:, span])
            add("q", tile, d_q[span])
            add("o", tile, mixed[span])
        for tile in range(first, last):
            span = slice(tile * LANES, (tile + 1) * LANES)
            if (head + 2) * size >= (tile + 1) * LANES:
                dv_ref[b, :, span] = sums.pop(("v", tile)).astype(BF16)
                dk_ref[b, :, span] = sums.pop(("k", tile)).astype(BF16)
                dq_ref[b, :, span] = sums.pop(("q", tile)).astype(BF16).T
                attnt_ref[b, span, :] = sums.pop(("o", tile)).astype(BF16)


def routed_copies(where_ref, refs, wq, wo, sems):
    g, z, c = where_ref[0], where_ref[1], where_ref[2]
    half_rows, wide, narrow = refs[0].shape[1], wq.shape[2], wo.shape[2] // 2
    groups = [(2 + 8 * i + 2 * other, other, step) for i, step in enumerate((3, 2, 1)) for other in range(4)]
    by_kind = []
    for far in range(2):
        kind = (g // 2) ^ far
        first, second = [], []
        for side in range(2):
            half = (g % 2) ^ side
            found = [(refs[i], 2 * kind + half, 2 * z + core) for i, core in ((0, c), (1, 1 - c))]
            for i, other, step in groups:
                if other == 2 * far + side:
                    chip = 2 * lax.rem(z + step, 4)
                    found += [(refs[i], 0, chip + c), (refs[i + 1], 0, chip + 1 - c)]
            for ref, at, shard in found:
                row = pl.multiple_of((shard * 2 + half) * half_rows, 16)
                out_row = pl.multiple_of(shard * half_rows, 16)
                column = pl.multiple_of(half * narrow, LANES)
                first.append(
                    pltpu.make_async_copy(
                        ref.at[at, :, pl.ds(0, wide)],
                        wq.at[kind, pl.ds(row, half_rows), :],
                        sems.at[far, len(first)],
                    )
                )
                second.append(
                    pltpu.make_async_copy(
                        ref.at[at, :, pl.ds(wide, narrow)],
                        wo.at[kind, pl.ds(out_row, half_rows), pl.ds(column, narrow)],
                        sems.at[far, 16 + len(second)],
                    )
                )
        by_kind.append(first + second)
    return by_kind


def weight_copies(routed, where_ref, refs, wq, wo, sems):
    if routed:
        return routed_copies(where_ref, refs, wq, wo, sems)
    return [
        [
            pltpu.make_async_copy(ref.at[kind], to.at[kind], sems.at[kind, i])
            for i, (ref, to) in enumerate(zip(refs, (wq, wo)))
        ]
        for kind in range(2)
    ]


def by_encoder(routed, where_ref, kind_ref, copies, body):
    for group in copies:
        for copy in group:
            copy.start()
    blocks = kind_ref.shape[0]
    first = where_ref[0] // 2 if routed else 0

    def step(i, carry):
        b, far = lax.rem(i, blocks), lax.div(i, blocks)
        for turn, group in enumerate(copies):

            @pl.when(i == turn * blocks)
            def _():
                for copy in group:
                    copy.wait()

        kind = first ^ far

        @pl.when(kind_ref[b] == kind)
        def _():
            body(b, kind)

        return carry

    lax.fori_loop(0, 2 * blocks, step, 0)


def layer_kernel(routed, n_weights, where_ref, kind_ref, h_ref, cot_ref, *rest):
    weights, rest = rest[:n_weights], rest[n_weights:]
    attnt_ref, dq_ref, dk_ref, dv_ref, wq, wo, qkv_ref, da_ref, sems = rest
    chunk = 3 * LANES

    def body(b, kind):
        for at in range(0, wq.shape[2], chunk):
            qkv_ref[:, at : at + chunk] = dot_nn(h_ref[b], wq[kind, :, at : at + chunk]).astype(BF16)
        for at in range(0, wo.shape[1], LANES):
            da_ref[:, at : at + LANES] = dot_nt(cot_ref[b], wo[kind, at : at + LANES, :]).astype(BF16)

        @pl.when(kind == 0)
        def _():
            attend(b, A_HEADS, A_SIZE, qkv_ref.shape[0], qkv_ref, da_ref, attnt_ref, dq_ref, dk_ref, dv_ref)

        @pl.when(kind != 0)
        def _():
            attend(b, V_HEADS, V_SIZE, VWIN, qkv_ref, da_ref, attnt_ref, dq_ref, dk_ref, dv_ref)

    by_encoder(routed, where_ref, kind_ref, weight_copies(routed, where_ref, weights, wq, wo, sems), body)


def result_kernel(routed, n_weights, where_ref, kind_ref, rank_ref, x_ref, cot_ref, gain_ref, attnt_ref, dq_ref, dk_ref, dv_ref, *rest):
    weights, rest = rest[:n_weights], rest[n_weights:]
    encoded_ref, grad_ref, wq, wo, wide_ref, sems = rest
    inner = dq_ref.shape[2]
    chunk = 2 * LANES
    width = x_ref.shape[2]

    def body(b, kind):
        rank = rank_ref[b]
        attn = attnt_ref[b].T
        for at in range(0, width, chunk):
            span = slice(at, at + chunk)
            encoded_ref[rank, :, span] = (
                x_ref[b, :, span].astype(F32) + dot_nn(attn, wo[kind, :, span])
            ).astype(BF16)
            wide_ref[:, span] = (
                dot_nt(dq_ref[b], wq[kind, span, :inner])
                + dot_nt(dk_ref[b], wq[kind, span, inner : 2 * inner])
                + dot_nt(dv_ref[b], wq[kind, span, 2 * inner :])
            )
        x_hat, inverse = normalise(x_ref[b].astype(F32))
        scaled = wide_ref[...] * gain_ref[pl.ds(kind, 1), :]
        d_input = inverse * (
            scaled
            - jnp.mean(scaled, axis=-1, keepdims=True)
            - x_hat * jnp.mean(scaled * x_hat, axis=-1, keepdims=True)
        )
        grad_ref[rank] = (cot_ref[b].astype(F32) + d_input).astype(BF16)

    by_encoder(routed, where_ref, kind_ref, weight_copies(routed, where_ref, weights, wq, wo, sems), body)


def left_kernel(where_ref, kind_ref, ht_a, ht_b, left):
    g, c = where_ref[0], where_ref[2]
    count = ht_a.shape[0]
    rows = left.shape[2] // 8
    for far in range(2):
        kind = (g // 2) ^ far
        for i in range(2 * count):
            source = ht_a if i < count else ht_b
            keep = kind_ref[i] == kind
            for side in range(2):
                for z in range(4):
                    row = pl.multiple_of(((2 * z + c) * 2 + ((g % 2) ^ side)) * rows, 16)
                    value = source[i % count, pl.ds(row, rows), :]
                    at = (side * 4 + z) * rows
                    left[far, i // count, at : at + rows, (i % count) * LANES : (i % count + 1) * LANES] = (
                        jnp.where(keep, value, jnp.zeros_like(value))
                    )


def out_terms_kernel(where_ref, kind_ref, attnt_a, attnt_b, cot_a, cot_b, own_ref, far_ref, sent_ref, left):
    g, z, c = where_ref[0], where_ref[1], where_ref[2]
    count = attnt_a.shape[0]
    rows = left.shape[2] // 4
    half_width = cot_a.shape[2] // 2
    for far in range(2):
        kind = (g // 2) ^ far
        for i in range(2 * count):
            source = attnt_a if i < count else attnt_b
            keep = kind_ref[i] == kind
            for step in range(4):
                row = pl.multiple_of((2 * (z ^ step) + c) * rows, 16)
                value = source[i % count, pl.ds(row, rows), :]
                left[far, i // count, step * rows : (step + 1) * rows, (i % count) * LANES : (i % count + 1) * LANES] = (
                    jnp.where(keep, value, jnp.zeros_like(value))
                )
    for far in range(2):
        for side in range(2):
            span = pl.ds(pl.multiple_of(((g % 2) ^ side) * half_width, LANES), half_width)
            total = dot_nn(left[far, 0], cot_a[:, :, span].reshape(-1, half_width))
            total += dot_nn(left[far, 1], cot_b[:, :, span].reshape(-1, half_width))
            total = total.reshape(4, rows, half_width)
            own_ref[2 * far + side] = total[0]
            far_ref[2 * far + side] = total[2]
            sent_ref[0, 2 * far + side] = total[1].astype(BF16)
            sent_ref[1, 2 * far + side] = total[3].astype(BF16)


def qkv_terms_kernel(left, *rest):
    pairs, (y_ref, x_ref, own_ref, xa_ref, yb_ref) = rest[:6], rest[6:]
    rows = left.shape[2] // 8
    width, cut = pairs[0].shape[2], xa_ref.shape[2]
    chunk = 3 * LANES
    for far in range(2):
        for part in range(3):
            d_a, d_b = pairs[2 * part : 2 * part + 2]
            for low in range(0, width, chunk):
                size = min(chunk, width - low)
                span = slice(low, low + size)
                total = dot_nn(left[far, 0], d_a[:, :, span].reshape(-1, size))
                total += dot_nn(left[far, 1], d_b[:, :, span].reshape(-1, size))
                total = total.reshape(2, 4, rows, size)
                at = part * width + low
                first = slice(at, at + size)
                last = slice(at - cut, at - cut + size)
                if far == 0:
                    own_ref[:, :, first] = total[0]
                for side in range(2):
                    if (far, side) == (0, 0):
                        continue
                    if at < cut and far:
                        y_ref[side, :, :, first] = total[side].astype(BF16)
                    elif at < cut:
                        xa_ref[:, :, first] = total[side]
                    elif side:
                        x_ref[far, :, :, last] = total[side].astype(BF16)
                    else:
                        yb_ref[:, :, last] = total[side]


QKV_CUT = 1024
STEPS = ((slice(0, 512), slice(0, 512)), (slice(512, None), slice(512, None)))
OUT_CUT = 384


def left_factor(where, kinds, ht, ht_other):
    count, width, window = ht.shape
    return pl.pallas_call(
        left_kernel,
        out_shape=jax.ShapeDtypeStruct((2, 2, width // 2, count * window), BF16),
        in_specs=[SMEM, SMEM] + [VMEM] * 2,
        out_specs=VMEM,
        compiler_params=params(),
        cost_estimate=cost(0.01),
        name="left_factor",
    )(where, kinds, ht, ht_other)


def out_terms(where, kinds, *pairs):
    count, inner, window = pairs[0].shape
    rows, width = inner // 8, pairs[2].shape[2] // 2
    return pl.pallas_call(
        out_terms_kernel,
        out_shape=[
            jax.ShapeDtypeStruct((4, rows, width), F32),
            jax.ShapeDtypeStruct((4, rows, width), F32),
            jax.ShapeDtypeStruct((2, 4, rows, width), BF16),
        ],
        in_specs=[SMEM, SMEM] + [VMEM] * len(pairs),
        out_specs=[VMEM] * 3,
        scratch_shapes=[pltpu.VMEM((2, 2, inner // 2, count * window), BF16)],
        compiler_params=params(),
        cost_estimate=cost(0.01),
        name="out_terms",
    )(where, kinds, *pairs)


def qkv_terms(left, *pairs):
    rows, columns = left.shape[2] // 8, 3 * pairs[0].shape[2]
    rest = columns - QKV_CUT
    return pl.pallas_call(
        qkv_terms_kernel,
        out_shape=[
            jax.ShapeDtypeStruct((2, 4, rows, QKV_CUT), BF16),
            jax.ShapeDtypeStruct((2, 4, rows, rest), BF16),
            jax.ShapeDtypeStruct((4, rows, columns), F32),
            jax.ShapeDtypeStruct((4, rows, QKV_CUT), F32),
            jax.ShapeDtypeStruct((4, rows, rest), F32),
        ],
        in_specs=[VMEM] * (1 + len(pairs)),
        out_specs=[VMEM] * 5,
        compiler_params=params(),
        cost_estimate=cost(0.01),
        name="qkv_terms",
    )(left, *pairs)


def flat(groups, shards, move):
    pairs = []
    for g in range(groups):
        for d in range(shards):
            to_g, to_d = move(g, d)
            pairs.append((g * shards + d, to_g * shards + to_d))
    return pairs


def routes(groups, shards):
    chips = shards // 2
    make = functools.partial(flat, groups, shards)
    return {
        "sibling": make(lambda g, d: (g, d ^ 1)),
        "x": make(lambda g, d: (g ^ 1, d)),
        "y": make(lambda g, d: (g ^ 2, d)),
        "z1": make(lambda g, d: (g, d ^ 2)),
        "z2": make(lambda g, d: (g, d ^ 4)),
        "z": [
            make(lambda g, d, s=s: (g, (d // 2 + s) % chips * 2 + d % 2)) for s in range(chips)
        ],
    }


def send(value, route):
    return lax.ppermute(value, AXES, route)


def tied(value, *others):
    return lax.optimization_barrier((value, *others))[0]


def gather_small(norm_gain, modality, route, z, c):
    kinds, rows = norm_gain.shape
    gains = norm_gain.astype(F32).reshape(1, -1)
    sibling = send(jnp.concatenate([gains, modality.astype(F32)[None]], axis=1), route["sibling"])
    others, kinds_other = sibling[:, : kinds * rows], sibling[0, kinds * rows :].astype(jnp.int32)
    pair = jnp.concatenate([jnp.where(c == 0, gains, others), jnp.where(c == 0, others, gains)], axis=0)
    chips = jnp.arange(4)[:, None, None]
    total = jnp.where(chips == z, pair[None], 0)
    for step in range(1, 4):
        total += jnp.where(chips == (z + 4 - step) % 4, send(pair, route["z"][step])[None], 0)
    return total.reshape(8, kinds, rows).transpose(1, 0, 2).reshape(kinds, -1), kinds_other


def quarter_of(qkv_weight, out_weight, q):
    rows, narrow = qkv_weight.shape[1] // 2, out_weight.shape[2] // 2
    own_qkv = lax.dynamic_slice(qkv_weight, (q // 2, q % 2 * rows, 0), (1, rows, qkv_weight.shape[2]))
    own_out = lax.dynamic_slice(out_weight, (q // 2, 0, q % 2 * narrow), (1, out_weight.shape[1], narrow))
    return jnp.concatenate([own_qkv, own_out], axis=2)


def quarters_of(qkv_weight, out_weight):
    kinds, rows, columns = qkv_weight.shape
    narrow = out_weight.shape[2] // 2
    return jnp.concatenate(
        [
            qkv_weight.reshape(4, rows // 2, columns),
            out_weight.reshape(kinds, -1, 2, narrow).transpose(0, 2, 1, 3).reshape(4, -1, narrow),
        ],
        axis=2,
    )


def send_terms(terms, route):
    to_y, to_x = terms[:2]
    return send(to_y, route["y"]), send(to_x, route["x"])


def reduce_plane(terms, arrived, route):
    _, _, own, x_term, y_term = terms
    from_y, from_x = arrived
    next_x = send((x_term + from_y[1].astype(F32)).astype(BF16), route["x"])
    next_y = send((y_term + from_x[1].astype(F32)).astype(BF16), route["y"])
    return own + jnp.concatenate(
        [
            from_y[0].astype(F32) + next_x.astype(F32),
            from_x[0].astype(F32) + next_y.astype(F32),
        ],
        axis=-1,
    )


def line_parts(total, z):
    parts = [lax.dynamic_index_in_dim(total, (z + step) % 4, 0, keepdims=False) for step in range(4)]
    return [parts[0]] + [part.astype(BF16) for part in parts[1:]]


def send_line(parts, route):
    return [send(parts[step], route["z"][step]) for step in range(1, 4)]


def add_line(own, arrived):
    return own + sum(part.astype(F32) for part in arrived)


def plane_terms(total, cut):
    first, second = total[..., :cut], total[..., cut:]
    return [
        first[2:].astype(BF16),
        jnp.stack([second[1], second[3]]).astype(BF16),
        total[0],
        first[1],
        second[2],
    ]


def both_halves(share, g, route):
    other = send(share.astype(BF16), route["x"]).astype(F32)
    return [jnp.where(g % 2 == i, share, other) for i in range(2)]


def whole_weights(qkv_weight, out_weight):
    return [
        lax.all_gather(qkv_weight, "dp", axis=1, tiled=True),
        lax.all_gather(out_weight, "dp", axis=1, tiled=True),
    ]


def summed_terms(kinds, h, dqkv, attn, cot):
    shards = lax.axis_size("dp")
    results = []
    for left, right in ((h, dqkv), (attn, cot)):
        parts = []
        for kind in range(2):
            keep = (kinds == kind)[:, None, None]
            parts.append(
                jnp.einsum("bwi,bwj->ij", jnp.where(keep, left, 0), right, preferred_element_type=F32)
            )
        total = lax.psum_scatter(
            jnp.stack(parts).reshape(2, shards, -1, right.shape[2]), "dp", scatter_dimension=1
        )
        total = lax.psum(total, "grp")
        results.append(lax.dynamic_index_in_dim(total, lax.axis_index("grp") // 2, 0, keepdims=False))
    return results


def shards(blocks, cotangent, modality, time_rank, qkv_weight, out_weight, norm_gain):
    groups, shard_count = lax.axis_size("grp"), lax.axis_size("dp")
    g, d = lax.axis_index("grp"), lax.axis_index("dp")
    z, c = d // 2, d % 2
    count, window, width = blocks.shape
    columns = qkv_weight.shape[2]
    inner = columns // 3
    routed = groups == 4 and shard_count == 8 and out_weight.shape[1] % 16 == 0
    where = jnp.stack([g, z, c]).astype(jnp.int32)
    rows = count * window

    def normed(blocks, gain):
        return pl.pallas_call(
            norm_kernel,
            out_shape=[
                jax.ShapeDtypeStruct(blocks.shape, BF16),
                jax.ShapeDtypeStruct((count, width, window), BF16),
            ],
            in_specs=[SMEM, VMEM, VMEM],
            out_specs=[VMEM] * 2,
            compiler_params=params(),
            cost_estimate=cost(0.01),
            name="norm",
        )(modality, blocks, gain)

    if routed:
        route = routes(groups, shard_count)

        def in_plane(held):
            return send(held, route["x"]), send(held, route["y"])

        def sibling(value, *after):
            return send(tied(value, *after) if after else value, route["sibling"])

        own = quarter_of(qkv_weight, out_weight, g)
        near = send(own, route["z"][1])
        gain, kinds_other = gather_small(tied(norm_gain, own), modality, route, z, c)
        near = tied(near, gain)
        far = send(near, route["z"][1])
        near_x, near_y = in_plane(near)
        h, ht = normed(tied(blocks, near), gain)
        quarters = quarters_of(tied(qkv_weight, near), out_weight)
        diagonal = lax.dynamic_slice_in_dim(quarters, g ^ 3, 1, 0)
        quarters_other = sibling(quarters)
        cot_other = sibling(cotangent, near)
        far = tied(far, near_x, near_y, h, quarters_other)
        far_x, far_y = in_plane(far)
        back = send(tied(own, far), route["z"][3])
        kinds = jnp.concatenate([modality, kinds_other])
        ht_other = sibling(ht, far)
        left = left_factor(where, kinds, ht, ht_other)
        near_other = sibling(near, far)
        near_x_other = sibling(near_x, near_other)
        near_y_other = sibling(near_y, near_other)
        back = tied(back, far_x, far_y, left, near_other)
        back_x, back_y = in_plane(back)
        near_across = send(tied(diagonal, back), route["z"][1])
        far_other = sibling(far, back)
        far_x_other = sibling(far_x, far_other)
        far_y_other = sibling(far_y, far_other)
        back_other = sibling(back, far_other)
        far_across = send(tied(far_x, back), route["y"])
        back_across = send(tied(diagonal, back), route["z"][3])
        weights = [quarters, quarters_other, near, near_other, near_x, near_x_other, near_y, near_y_other]
        weights += [near_across, sibling(near_across), far, far_other, far_x, far_x_other, far_y, far_y_other]
        weights += [far_across, sibling(far_across), back, back_other, back_x, sibling(back_x)]
        weights += [back_y, sibling(back_y), back_across, sibling(back_across)]
    else:
        gain = lax.all_gather(norm_gain, "dp", axis=1, tiled=True).astype(F32)
        weights = whole_weights(qkv_weight, out_weight)
        h, ht = normed(blocks, gain)
    n_weights = len(weights)
    weight_scratch = [
        pltpu.VMEM((2, width, columns), BF16),
        pltpu.VMEM((2, inner, width), BF16),
    ]
    weight_sems = pltpu.SemaphoreType.DMA((2, 32))

    attnt, dq, dk, dv = pl.pallas_call(
        functools.partial(layer_kernel, routed, n_weights),
        out_shape=[jax.ShapeDtypeStruct((count, inner, window), BF16)]
        + [jax.ShapeDtypeStruct((count, window, inner), BF16)] * 3,
        in_specs=[SMEM, SMEM, VMEM, VMEM] + [HBM] * n_weights,
        out_specs=[VMEM] * 4,
        scratch_shapes=weight_scratch
        + [pltpu.VMEM((window, columns), BF16), pltpu.VMEM((window, inner), BF16), weight_sems],
        compiler_params=params(),
        cost_estimate=cost(0.01),
        name="layer",
    )(where, modality, h, cotangent, *weights)

    def results(attnt):
        return pl.pallas_call(
            functools.partial(result_kernel, routed, n_weights),
            out_shape=[jax.ShapeDtypeStruct(blocks.shape, BF16)] * 2,
            in_specs=[SMEM] * 3 + [VMEM] * 7 + [HBM] * n_weights,
            out_specs=[VMEM] * 2,
            scratch_shapes=weight_scratch + [pltpu.VMEM((window, width), F32), weight_sems],
            compiler_params=params(),
            cost_estimate=cost(0.01),
            name="result",
        )(where, modality, time_rank, blocks, cotangent, gain, attnt, dq, dk, dv, *weights)

    if routed:
        dq_other, dk_other, dv_other, attnt_other = [
            send(part, route["sibling"]) for part in (dq, dk, dv, attnt)
        ]
        terms = qkv_terms(left, dq, dq_other, dk, dk_other, dv, dv_other)
        arrived = send_terms(terms, route)
        out_own, out_far, out_sent = out_terms(
            where, kinds, tied(attnt, terms[0]), attnt_other, cotangent, cot_other
        )
        out_near = send(out_sent, route["z1"])
        encoded, block_grad = results(tied(attnt, out_own))
        out_near = tied(out_near, encoded)
        out_value = (out_far + out_near[1].astype(F32)).astype(BF16)
        *arrived, out_value = lax.optimization_barrier((*arrived, out_value))
        out_next = send(out_value, route["z2"])
        parts = []
        for first, last in STEPS:
            step_arrived = (arrived[0][..., first], arrived[1][..., last])
            own = jnp.concatenate([terms[2][..., :QKV_CUT][..., first], terms[2][..., QKV_CUT:][..., last]], axis=2)
            step_terms = (None, None, own, terms[3][..., first], terms[4][..., last])
            parts.append(line_parts(reduce_plane(step_terms, step_arrived, route), z))
        shares = [add_line(part[0], send_line(part, route)) for part in parts]
        out_total = tied(out_own + out_near[0].astype(F32) + out_next.astype(F32), *parts[1])
        terms = plane_terms(out_total, OUT_CUT)
        share = reduce_plane(terms, send_terms(terms, route), route)
        share_out = jnp.concatenate(both_halves(share, g, route), axis=1)
        (first_a, first_b), (last_a, last_b) = [
            tuple(zip(*[(half[:, :512], half[:, 512:]) for half in both_halves(share, g, route)]))
            for share in shares
        ]
        share_qkv = jnp.concatenate(
            [jnp.concatenate(halves, axis=0) for halves in (first_a, last_a, first_b, last_b)], axis=1
        )
    else:
        encoded, block_grad = results(attnt)
        share_qkv, share_out = summed_terms(
            modality, h, jnp.concatenate([dq, dk, dv], axis=2), attnt.transpose(0, 2, 1), cotangent
        )

    kind = g // 2
    own_weight = lax.dynamic_index_in_dim(qkv_weight, kind, 0, keepdims=False).astype(F32)
    own_gain = lax.dynamic_index_in_dim(norm_gain, kind, 0, keepdims=False).astype(F32)
    share_gain = jnp.sum(share_qkv * own_weight, axis=1) / own_gain

    return (encoded, block_grad, share_qkv[None], share_out[None], share_gain[None])


def solution(mesh):
    return jax.shard_map(
        shards,
        mesh=mesh,
        in_specs=(
            P(("grp", "dp"), None, None),
            P(("grp", "dp"), None, None),
            P(("grp", "dp")),
            P(("grp", "dp")),
            P(None, "dp", None),
            P(None, "dp", None),
            P(None, "dp"),
        ),
        out_specs=(
            P(("grp", "dp"), None, None),
            P(("grp", "dp"), None, None),
            P("grp", "dp", None),
            P("grp", "dp", None),
            P("grp", "dp"),
        ),
        check_vma=False,
    )
```
